32 devices in a mesh: dp: 4 (over z), ctx: 8 (over y, x, core).
Axes of the slice: x: 2, y: 2, z: 4, core: 2. Of those that a mesh axis runs over, the one named last changes fastest.
Arguments:
- tokens: bfloat16 [4, 1024, 2048], P('dp', 'ctx'), may hold values from -6 to 6
- cotangent: bfloat16 [4, 1024, 2048], P('dp', 'ctx'), may hold values from -6 to 6
- block_ids: int32 [16], replicated, may hold values from 0 to 15, as said below
- attn_weight: float32 [2048, 8192], P(('dp', 'ctx')), may hold values from -1.06066017 to 1.06066017
- gate_up: float32 [2048, 16384], P(('dp', 'ctx')), may hold values from -0.125 to 0.125
- down_weight: float32 [8192, 2048], P(('dp', 'ctx')), may hold values from -0.0625 to 0.0625
- norm_gains: float32 [2, 2048], P(None, ('dp', 'ctx')), may hold values from 0.25 to 1.75
- attn_first: float32 [2048, 8192], P(('dp', 'ctx')), may hold values from -25.6 to 25.6
- attn_second: float32 [2048, 8192], P(('dp', 'ctx')), may hold values from 2.048 to 311.296
- gate_first: float32 [2048, 16384], P(('dp', 'ctx')), may hold values from -12.8 to 12.8
- gate_second: float32 [2048, 16384], P(('dp', 'ctx')), may hold values from 19.6608 to 77.824
- down_first: float32 [8192, 2048], P(('dp', 'ctx')), may hold values from -25.6 to 25.6
- down_second: float32 [8192, 2048], P(('dp', 'ctx')), may hold values from 77.824 to 311.296
- gain_first: float32 [2, 2048], P(None, ('dp', 'ctx')), may hold values from -42.24 to 42.24
- gain_second: float32 [2, 2048], P(None, ('dp', 'ctx')), may hold values from 217.088 to 860.16
Outputs:
- activations: bfloat16 [4, 1024, 2048], P('dp', 'ctx')
- input_grad: bfloat16 [4, 1024, 2048], P('dp', 'ctx')
- attn_grad: float32 [2048, 8192], P(('dp', 'ctx'))
- gate_grad: float32 [2048, 16384], P(('dp', 'ctx'))
- down_grad: float32 [8192, 2048], P(('dp', 'ctx'))
- gain_grad: float32 [2, 2048], P(None, ('dp', 'ctx'))
- attn_new: float32 [2048, 8192], P(('dp', 'ctx'))
- gate_new: float32 [2048, 16384], P(('dp', 'ctx'))
- down_new: float32 [8192, 2048], P(('dp', 'ctx'))
- gain_new: float32 [2, 2048], P(None, ('dp', 'ctx'))
- attn_moment: float32 [2048, 8192], P(('dp', 'ctx'))
- gate_moment: float32 [2048, 16384], P(('dp', 'ctx'))
- down_moment: float32 [8192, 2048], P(('dp', 'ctx'))
- gain_moment: float32 [2, 2048], P(None, ('dp', 'ctx'))
- attn_square: float32 [2048, 8192], P(('dp', 'ctx'))
- gate_square: float32 [2048, 16384], P(('dp', 'ctx'))
- down_square: float32 [8192, 2048], P(('dp', 'ctx'))
- gain_square: float32 [2, 2048], P(None, ('dp', 'ctx'))
The draws below stay inside these ranges and needn't reach their ends.
Inputs may be any that keep to these rules, and one draw needn't show every extreme that they name: `block_ids`: slots 2c and 2c + 1 (the rows of device c of ctx) hold a block b and the block 15 - b; every block of a sequence appears once, the same for all sequences.
All inputs are finite; a program needn't handle non-finite values.
Results may differ from the reference program's by a relative error of at most 0.015.
Values may be sent and summed in bfloat16 or wider, within the bound.
No kernel may reach another device: no remote copies, remote signals or barrier semaphores. Data moves between devices by JAX's collectives and lax.ppermute only.
A program may use at most 704 MiB of HBM per device.

```python
import math
import jax
import jax.numpy as jnp
from jax import lax

D = 2048
HEADS = 32
HEAD = 64
FF = 8192
STEP = 5
SEQ = 1024
SEQS = 4
TOKENS = 4096
BLOCK = 64


def column_scale(first, second):
    columns = jnp.arange(4 * D)
    return jnp.where(columns < 3 * D, first, second)[None, :].astype(jnp.float32)


def draw_block_ids(key, part):
    key = jax.random.fold_in(key, 1)
    count = SEQ // BLOCK // 2
    order = jax.random.permutation(jax.random.fold_in(key, 2), count).astype(jnp.int32)
    flips = jax.random.randint(jax.random.fold_in(key, 3), (count,), 0, 2)
    mirror = SEQ // BLOCK - 1 - order
    first = jnp.where(flips == 1, mirror, order)
    second = jnp.where(flips == 1, order, mirror)
    return jnp.stack([first, second], axis=1).reshape(-1).astype(jnp.int32)


def draw_attn_weight(key, part):
    key = jax.random.fold_in(key, 11)
    base = jax.random.truncated_normal(key, -6.0, 6.0, (D, 4 * D), jnp.float32)
    return base * column_scale(D ** (-0.5), 8.0 * D ** (-0.5))


def draw_attn_first(key, part):
    key = jax.random.fold_in(key, 12)
    base = jax.random.truncated_normal(key, -6.0, 6.0, (D, 4 * D), jnp.float32)
    return base * column_scale(0.6, 0.1) * (0.11 * TOKENS ** 0.5)


def draw_attn_second(key, part):
    key = jax.random.fold_in(key, 13)
    spread = jax.random.uniform(key, (D, 4 * D), jnp.float32, jnp.log(0.053), jnp.log(0.21))
    return jnp.exp(spread) * column_scale(0.36, 0.01) * TOKENS


def block_levels(key, extent, shards, least, top_value):
    loudness = 1.0
    for dim, parts in shards:
        heights = jax.random.uniform(jax.random.fold_in(jax.random.fold_in(key, 6), dim), (parts,), jnp.float32, least / len(shards), top_value / len(shards))
        loudness = loudness * jnp.repeat(jnp.exp(heights), extent[dim] // parts).reshape((-1,) + (1,) * (len(extent) - 1 - dim))
    return loudness


def gaussian(own_key, extent, width, bound, shards=(), held_as=jnp.bfloat16):
    gain = block_levels(own_key, extent, shards, -0.22, 0.18) if shards else 1.0
    result = jax.random.normal(own_key, extent, jnp.float32) * width * gain
    return jnp.minimum(jnp.maximum(result, -bound), bound).astype(held_as)


def setup_inputs(seed: int = 0) -> dict:
    seeds = jax.random.split(jax.random.key(seed), 16)
    tokens = gaussian(seeds[0], (SEQS, SEQ, D), 1.0, 6.0, ((0, 4), (1, 8)))
    cotangent = gaussian(seeds[1], (SEQS, SEQ, D), 1.0, 6.0, ((0, 4), (1, 8)))
    block_ids = draw_block_ids(jax.random.fold_in(seeds[15], 71), 0)
    attn_weight = draw_attn_weight(jax.random.fold_in(seeds[15], 71), 0)
    gate_up = gaussian(seeds[4], (D, 2 * FF), D ** -0.5, 0.125, ((0, 32),), jnp.float32)
    down_weight = gaussian(seeds[5], (FF, D), FF ** -0.5, 0.0625, ((0, 32),), jnp.float32)
    norm_gains = jnp.clip(1.0 + 0.15 * jax.random.normal(seeds[6], (2, D), jnp.float32), 0.25, 1.75)
    attn_first = draw_attn_first(jax.random.fold_in(seeds[15], 71), 0)
    attn_second = draw_attn_second(jax.random.fold_in(seeds[15], 71), 0)
    gate_first = gaussian(seeds[9], (D, 2 * FF), (0.033 * TOKENS ** 0.5), 12.8, ((0, 32),), jnp.float32)
    gate_second = jnp.clip(jnp.exp(math.log(77.824) - 1.375823 * jax.random.uniform(seeds[10], (D, 2 * FF), jnp.float32) ** block_levels(seeds[10], (D, 2 * FF), ((0, 32),), -0.2, 0.2)), 19.6608, 77.824)
    down_first = gaussian(seeds[11], (FF, D), (0.066 * TOKENS ** 0.5), 25.6, ((0, 32),), jnp.float32)
    down_second = jnp.clip(jnp.exp(math.log(311.296) - 1.3862944 * jax.random.uniform(seeds[12], (FF, D), jnp.float32) ** block_levels(seeds[12], (FF, D), ((0, 32),), -0.2, 0.2)), 77.824, 311.296)
    gain_first = gaussian(seeds[13], (2, D), (0.11 * TOKENS ** 0.5), 42.24, ((1, 32),), jnp.float32)
    gain_second = jnp.clip(jnp.exp(math.log(860.16) - 1.3768156 * jax.random.uniform(seeds[14], (2, D), jnp.float32) ** block_levels(seeds[14], (2, D), ((1, 32),), -0.2, 0.2)), 217.088, 860.16)
    return {"tokens": tokens, "cotangent": cotangent, "block_ids": block_ids, "attn_weight": attn_weight, "gate_up": gate_up, "down_weight": down_weight, "norm_gains": norm_gains, "attn_first": attn_first, "attn_second": attn_second, "gate_first": gate_first, "gate_second": gate_second, "down_first": down_first, "down_second": down_second, "gain_first": gain_first, "gain_second": gain_second}


@jax.custom_vjp
def low(v):
    return lax.optimization_barrier(v.astype(jnp.bfloat16)).astype(jnp.float32)

@jax.custom_vjp
def low_back(v):
    return v

def low_keep(v):
    return (low(v), None)

def low_pass(kept, grad):
    return (grad,)

def back_keep(v):
    return (v, None)

def back_low(kept, grad):
    return (low(grad),)
low.defvjp(low_keep, low_pass)
low_back.defvjp(back_keep, back_low)
norm_eps = 1e-05
rope_base = 130000.0
beta_one = 0.9
beta_two = 0.95
adam_eps = 1e-08
decay_rate = 0.1
gain_rate = 0.4
masked = -1e+30

def highest(first, second):
    return jnp.dot(first, second, precision=lax.Precision.HIGHEST, preferred_element_type=jnp.float32)

def rms_scale(values):
    return lax.rsqrt(lax.optimization_barrier(jnp.mean(values * values, axis=-1, keepdims=True)) + norm_eps)

def angles(positions):
    index = jnp.arange(HEAD // 2, dtype=jnp.float32)
    freqs = jnp.power(jnp.float32(rope_base), -2.0 * index / HEAD)
    phase = positions.astype(jnp.float32)[:, None] * freqs[None, :]
    phase = jnp.concatenate([phase, phase], axis=-1)
    return (jnp.cos(phase)[:, None, :], jnp.sin(phase)[:, None, :])

def rotate(values, cosine, sine):
    middle = values.shape[-1] // 2
    turned = jnp.concatenate([-values[..., middle:], values[..., :middle]], axis=-1)
    return values * cosine + turned * sine

def layer(inputs, attn_low, gate_low, down_low, gain_low, positions):
    seq_len = inputs.shape[0]
    scale = HEAD ** (-0.5)
    normed_one = inputs * rms_scale(inputs)
    hidden_one = low(normed_one * gain_low[0])
    projected = highest(hidden_one, attn_low[:, :3 * D])
    query_pre = low_back(projected[:, :D])
    key_pre = low_back(projected[:, D:2 * D])
    values = low(low_back(projected[:, 2 * D:])).reshape(seq_len, HEADS, HEAD)
    cosine, sine = angles(positions)
    queries = low(rotate(query_pre.reshape(seq_len, HEADS, HEAD), cosine, sine))
    keys = low(rotate(key_pre.reshape(seq_len, HEADS, HEAD), cosine, sine))
    block = 512 if seq_len % 512 == 0 else seq_len

    @jax.checkpoint
    def attend(pair):
        query_block, query_pos = pair
        scores = jnp.einsum('qhd,khd->hqk', query_block, keys, precision=lax.Precision.HIGHEST) * scale
        scores = low_back(scores)
        allowed = positions[None, :] <= query_pos[:, None]
        scores = jnp.where(allowed[None], scores, masked)
        peak = lax.optimization_barrier(jnp.max(scores, axis=-1, keepdims=True))
        weights = jnp.exp(scores - peak)
        weights = low(weights / lax.optimization_barrier(jnp.sum(weights, axis=-1, keepdims=True)))
        return jnp.einsum('hqk,khd->qhd', weights, values, precision=lax.Precision.HIGHEST)
    mixed = lax.map(attend, (queries.reshape(seq_len // block, block, HEADS, HEAD), positions.reshape(seq_len // block, block)))
    mixed = low(low_back(mixed.reshape(seq_len, D)))
    after = inputs + low_back(highest(mixed, attn_low[:, 3 * D:]))
    normed_two = after * rms_scale(after)
    hidden_two = low(normed_two * gain_low[1])
    gate_both = low_back(highest(hidden_two, gate_low))
    activation = low(jax.nn.silu(gate_both[:, :FF]) * gate_both[:, FF:])
    return after + low_back(highest(activation, down_low))

def adam_step(weight, grad, first, second, rate, decay):
    first = beta_one * first + (1.0 - beta_one) * grad
    second = beta_two * second + (1.0 - beta_two) * grad * grad
    corrected_first = first / (1.0 - beta_one ** STEP)
    corrected_second = second / (1.0 - beta_two ** STEP)
    fresh = weight - rate * (corrected_first / (jnp.sqrt(corrected_second) + adam_eps) + decay * weight)
    return (fresh, first, second)

def reference(tokens, cotangent, block_ids, attn_weight, gate_up, down_weight, norm_gains, attn_first, attn_second, gate_first, gate_second, down_first, down_second, gain_first, gain_second):
    positions = (block_ids[:, None] * BLOCK + jnp.arange(BLOCK, dtype=jnp.int32)[None, :]).reshape(-1)

    def forward(inputs, attn_full, gate_full, down_full, gain_full):
        attn_low = low(attn_full)
        gate_low = low(gate_full)
        down_low = low(down_full)
        gain_low = low(gain_full)
        single = jax.checkpoint(lambda row: layer(row, attn_low, gate_low, down_low, gain_low, positions))
        return lax.map(single, inputs)
    outputs, pullback = jax.vjp(forward, tokens.astype(jnp.float32), attn_weight, gate_up, down_weight, norm_gains)
    input_grad, attn_grad, gate_grad, down_grad, gain_grad = pullback(cotangent.astype(jnp.float32))
    attn_new, attn_moment, attn_square = adam_step(attn_weight, attn_grad, attn_first, attn_second, 3.0 / math.sqrt(D), decay_rate)
    gate_new, gate_moment, gate_square = adam_step(gate_up, gate_grad, gate_first, gate_second, 3.0 / math.sqrt(D), decay_rate)
    down_new, down_moment, down_square = adam_step(down_weight, down_grad, down_first, down_second, 3.0 / math.sqrt(FF), decay_rate)
    gain_new, gain_moment, gain_square = adam_step(norm_gains, gain_grad, gain_first, gain_second, gain_rate, 0.0)
    return (outputs.astype(jnp.bfloat16), input_grad.astype(jnp.bfloat16), attn_grad, gate_grad, down_grad, gain_grad, attn_new, gate_new, down_new, gain_new, attn_moment, gate_moment, down_moment, gain_moment, attn_square, gate_square, down_square, gain_square)
```

```python
import math

import jax
import jax.numpy as jnp
from jax import lax
from jax.sharding import PartitionSpec as P

D = 2048
HEADS = 32
HEAD = 64
FF = 8192
STEP = 5

norm_eps = 1e-05
rope_base = 130000.0
beta_one = 0.9
beta_two = 0.95
adam_eps = 1e-08
decay_rate = 0.1
gain_rate = 0.4
masked = -1e30

bf16 = jnp.bfloat16
f32 = jnp.float32


def rms_scale(values):
    return lax.rsqrt(jnp.mean(values * values, axis=-1, keepdims=True) + norm_eps)


def angles(positions):
    index = jnp.arange(HEAD // 2, dtype=f32)
    freqs = jnp.power(f32(rope_base), -2.0 * index / HEAD)
    phase = positions.astype(f32)[:, None] * freqs[None, :]
    phase = jnp.concatenate([phase, phase], axis=-1)
    return (jnp.cos(phase)[:, None, :], jnp.sin(phase)[:, None, :])


def rotate(values, cosine, sine):
    middle = values.shape[-1] // 2
    turned = jnp.concatenate([-values[..., middle:], values[..., :middle]], axis=-1)
    return values * cosine + turned * sine


def unrotate(values, cosine, sine):
    middle = values.shape[-1] // 2
    sined = values * sine
    turned = jnp.concatenate([sined[..., middle:], -sined[..., :middle]], axis=-1)
    return values * cosine + turned


def dot(first, second):
    return jnp.dot(first, second, preferred_element_type=f32)


def contract_last(first, second):
    return lax.dot_general(first, second, (((1,), (1,)), ((), ())), preferred_element_type=f32)


def contract_first(first, second):
    return lax.dot_general(first, second, (((0,), (0,)), ((), ())), preferred_element_type=f32)


def adam_step(weight, grad, first, second, rate, decay):
    first = beta_one * first + (1.0 - beta_one) * grad
    second = beta_two * second + (1.0 - beta_two) * grad * grad
    corrected_first = first / (1.0 - beta_one**STEP)
    corrected_second = second / (1.0 - beta_two**STEP)
    fresh = weight - rate * (
        corrected_first / (jnp.sqrt(corrected_second) + adam_eps) + decay * weight
    )
    return (fresh, first, second)


def gather(values, axis):
    return lax.all_gather(values, axis, axis=0, tiled=True)


def scatter(values, axis):
    return lax.psum_scatter(values, axis, scatter_dimension=0, tiled=True)


def exchange(pieces):
    return lax.all_to_all(pieces, "ctx", split_axis=0, concat_axis=0, tiled=True)


def attention_forward(queries, keys, values, positions, scale):
    scores = jnp.einsum("qhd,khd->hqk", queries, keys, preferred_element_type=f32) * scale
    allowed = positions[None, :] <= positions[:, None]
    scores = jnp.where(allowed[None], scores, masked)
    peak = jnp.max(scores, axis=-1, keepdims=True)
    weights = jnp.exp(scores - peak)
    total = jnp.sum(weights, axis=-1, keepdims=True)
    mixed = jnp.einsum(
        "hqk,khd->qhd", (weights / total).astype(bf16), values, preferred_element_type=f32
    )
    return mixed, peak + jnp.log(total)


def attention_backward(queries, keys, values, positions, scale, log_total, grad_mixed):
    scores = jnp.einsum("qhd,khd->hqk", queries, keys, preferred_element_type=f32) * scale
    allowed = positions[None, :] <= positions[:, None]
    probs = jnp.where(allowed[None], jnp.exp(scores - log_total), 0.0)
    grad_probs = jnp.einsum("qhd,khd->hqk", grad_mixed, values, preferred_element_type=f32)
    delta = jnp.sum(probs * grad_probs, axis=-1, keepdims=True)
    grad_scores = (probs * (grad_probs - delta)).astype(bf16)
    grad_query = jnp.einsum("hqk,khd->qhd", grad_scores, keys, preferred_element_type=f32) * scale
    grad_keys = jnp.einsum("hqk,qhd->khd", grad_scores, queries, preferred_element_type=f32) * scale
    grad_values = jnp.einsum(
        "hqk,qhd->khd", probs.astype(bf16), grad_mixed, preferred_element_type=f32
    )
    return grad_query, grad_keys, grad_values


def body(
    tokens,
    cotangent,
    block_ids,
    attn_weight,
    gate_up,
    down_weight,
    norm_gains,
    attn_first,
    attn_second,
    gate_first,
    gate_second,
    down_first,
    down_second,
    gain_first,
    gain_second,
):
    every = ("dp", "ctx")
    width = attn_weight.shape[1] // 4
    planes = lax.axis_size("dp")
    ranks = lax.axis_size("ctx")
    own_rows = attn_weight.shape[0]
    units = down_weight.shape[0]
    rows = tokens.shape[1]
    half = rows // 2
    seq_len = rows * ranks
    local_heads = HEADS // ranks
    local_width = local_heads * HEAD
    aligned = local_heads == planes
    rank = lax.axis_index("ctx")
    scale = HEAD ** (-0.5)
    positions = (
        block_ids[:, None] * half + jnp.arange(half, dtype=jnp.int32)[None, :]
    ).reshape(-1)
    cosine, sine = angles(positions)

    attn_low = attn_weight.astype(bf16)
    qkv_pieces = (
        attn_low[:, : 3 * width]
        .reshape(own_rows, 3, local_heads, ranks, HEAD)
        .transpose(3, 0, 1, 2, 4)
        .reshape(ranks, own_rows, 3 * local_width)
    )
    qkv = gather(exchange(qkv_pieces).reshape(ranks * own_rows, 3 * local_width), "dp")
    out_low = attn_low[:, 3 * width :]
    if aligned:
        out_proj = gather(out_low, "dp")
    else:
        out_all = gather(out_low, every).reshape(local_heads, ranks, HEAD, width)
        out_proj = lax.dynamic_index_in_dim(out_all, rank, 1, keepdims=False).reshape(
            local_width, width
        )
    gate_pieces = (
        gate_up.astype(bf16)
        .reshape(own_rows, 2, planes, ranks, units)
        .transpose(3, 0, 1, 2, 4)
        .reshape(ranks, own_rows, 2 * planes * units)
    )
    hidden = planes * units
    gate = gather(exchange(gate_pieces).reshape(ranks * own_rows, 2 * hidden), "dp")
    down = gather(down_weight.astype(bf16), "dp")

    gains_low = lax.all_gather(norm_gains.astype(bf16), every, axis=1, tiled=True)
    gain_one = gains_low[0].astype(f32)
    gain_two = gains_low[1].astype(f32)
    inputs_all = gather(tokens[0], "ctx").astype(f32)
    grad_out_all = gather(cotangent[0], "ctx")

    normed_all = inputs_all * rms_scale(inputs_all)
    hidden_one = (normed_all * gain_one).astype(bf16)
    projected = dot(hidden_one, qkv)
    by_head = projected.reshape(seq_len, 3, local_heads, HEAD)
    queries = rotate(by_head[:, 0], cosine, sine).astype(bf16)
    keys = rotate(by_head[:, 1], cosine, sine).astype(bf16)
    values = by_head[:, 2].astype(bf16)
    mixed, log_total = attention_forward(queries, keys, values, positions, scale)
    mixed_low = mixed.reshape(seq_len, local_width).astype(bf16)

    inputs = tokens[0].astype(f32)
    after = inputs + scatter(dot(mixed_low, out_proj).astype(bf16), "ctx").astype(f32)
    inv_two = rms_scale(after)
    normed_two = after * inv_two
    hidden_two = gather((normed_two * gain_two).astype(bf16), "ctx")
    gate_both = dot(hidden_two, gate)
    gate_part = gate_both[:, :hidden]
    up_part = gate_both[:, hidden:]
    gate_sigmoid = jax.nn.sigmoid(gate_part)
    gate_act = gate_part * gate_sigmoid
    activation = (gate_act * up_part).astype(bf16)
    outputs = after + scatter(dot(activation, down).astype(bf16), "ctx").astype(f32)

    grad_act = contract_last(grad_out_all, down)
    grad_gate = (
        grad_act * up_part * gate_sigmoid * (1.0 + gate_part * (1.0 - gate_sigmoid))
    ).astype(bf16)
    grad_up = (grad_act * gate_act).astype(bf16)
    grad_both = jnp.concatenate([grad_gate, grad_up], axis=1)
    grad_two = scatter(contract_last(grad_both, gate).astype(bf16), "ctx").astype(f32)
    down_grad = scatter(contract_first(activation, grad_out_all).astype(bf16), "dp").astype(f32)
    gate_term = scatter(contract_first(hidden_two, grad_both).astype(bf16), "dp")
    gate_grad = (
        exchange(gate_term.reshape(ranks, own_rows, 2 * hidden))
        .reshape(ranks, own_rows, 2, planes, units)
        .transpose(1, 2, 3, 0, 4)
        .reshape(own_rows, gate_up.shape[1])
        .astype(f32)
    )

    reduced_two = grad_two * gain_two
    grad_gain_two = jnp.sum(grad_two * normed_two, axis=0)
    grad_after = cotangent[0].astype(f32) + inv_two * (
        reduced_two - normed_two * jnp.mean(reduced_two * normed_two, axis=-1, keepdims=True)
    )
    after_low = gather(grad_after.astype(bf16), "ctx")
    grad_mixed = (
        contract_last(after_low, out_proj).astype(bf16).reshape(seq_len, local_heads, HEAD)
    )
    grad_query, grad_keys, grad_values = attention_backward(
        queries, keys, values, positions, scale, log_total, grad_mixed
    )
    grad_proj = jnp.concatenate(
        [
            unrotate(grad_query, cosine, sine).reshape(seq_len, local_width),
            unrotate(grad_keys, cosine, sine).reshape(seq_len, local_width),
            grad_values.reshape(seq_len, local_width),
        ],
        axis=1,
    ).astype(bf16)
    grad_one_part = contract_last(grad_proj, qkv)
    grad_gain_one = jnp.sum(grad_one_part * normed_all, axis=0)
    grad_one = scatter(grad_one_part.astype(bf16), "ctx").astype(f32)
    inv_one = rms_scale(inputs)
    normed_one = inputs * inv_one
    reduced_one = grad_one * gain_one
    grad_input = grad_after + inv_one * (
        reduced_one - normed_one * jnp.mean(reduced_one * normed_one, axis=-1, keepdims=True)
    )

    out_term = contract_first(mixed_low, after_low).astype(bf16)
    if aligned:
        out_grad = scatter(out_term, "dp").astype(f32)
    else:
        spread = jnp.zeros((local_heads, ranks, HEAD, width), bf16)
        spread = lax.dynamic_update_index_in_dim(
            spread, out_term.reshape(local_heads, 1, HEAD, width), rank, 1
        )
        out_grad = scatter(spread.reshape(HEADS * HEAD, width), every).astype(f32)
    qkv_term = scatter(contract_first(hidden_one, grad_proj).astype(bf16), "dp")
    qkv_grad = (
        exchange(qkv_term.reshape(ranks, own_rows, 3 * local_width))
        .reshape(ranks, own_rows, 3, local_heads, HEAD)
        .transpose(1, 2, 3, 0, 4)
        .reshape(own_rows, 3 * width)
        .astype(f32)
    )
    attn_grad = jnp.concatenate([qkv_grad, out_grad], axis=1)
    gain_grad = lax.psum_scatter(
        jnp.stack([grad_gain_one, grad_gain_two]), every, scatter_dimension=1, tiled=True
    )

    attn_new, attn_moment, attn_square = adam_step(
        attn_weight, attn_grad, attn_first, attn_second, 3.0 / math.sqrt(D), decay_rate
    )
    gate_new, gate_moment, gate_square = adam_step(
        gate_up, gate_grad, gate_first, gate_second, 3.0 / math.sqrt(D), decay_rate
    )
    down_new, down_moment, down_square = adam_step(
        down_weight, down_grad, down_first, down_second, 3.0 / math.sqrt(FF), decay_rate
    )
    gain_new, gain_moment, gain_square = adam_step(
        norm_gains, gain_grad, gain_first, gain_second, gain_rate, 0.0
    )
    return (
        outputs.astype(bf16)[None],
        grad_input.astype(bf16)[None],
        attn_grad,
        gate_grad,
        down_grad,
        gain_grad,
        attn_new,
        gate_new,
        down_new,
        gain_new,
        attn_moment,
        gate_moment,
        down_moment,
        gain_moment,
        attn_square,
        gate_square,
        down_square,
        gain_square,
    )


def solution(mesh):
    acts = P("dp", "ctx", None)
    weight = P(("dp", "ctx"), None)
    gains = P(None, ("dp", "ctx"))
    four = (weight, weight, weight, gains)
    return jax.shard_map(
        body,
        mesh=mesh,
        in_specs=(acts, acts, P()) + four + (weight,) * 6 + (gains,) * 2,
        out_specs=(acts, acts) + four * 4,
        check_vma=False,
    )
```

```python
import math

import jax
import jax.numpy as jnp
from jax import lax
from jax.experimental import pallas as pl
from jax.experimental.pallas import tpu as pltpu
from jax.sharding import PartitionSpec as P

D = 2048
HEADS = 32
HEAD = 64
FF = 8192
STEP = 5

norm_eps = 1e-05
rope_base = 130000.0
beta_one = 0.9
beta_two = 0.95
adam_eps = 1e-08
decay_rate = 0.1
gain_rate = 0.4
masked = -1e30
score_scale = HEAD ** (-0.5)
pair_width = 2 * HEAD
query_block = 256

bf16 = jnp.bfloat16
f32 = jnp.float32


def rms_scale(values):
    return lax.rsqrt(jnp.mean(values * values, axis=-1, keepdims=True) + norm_eps)


def angle_tables(positions):
    index = jnp.arange(HEAD // 2, dtype=f32)
    freqs = jnp.power(f32(rope_base), -2.0 * index / HEAD)
    phase = positions.astype(f32)[:, None] * freqs[None, :]
    return jnp.tile(jnp.cos(phase), (1, 4)), jnp.tile(jnp.sin(phase), (1, 4))


def dot(first, second, core=None):
    return jnp.dot(first, second, preferred_element_type=f32)


def contract_last(first, second, core=None):
    return lax.dot_general(first, second, (((1,), (1,)), ((), ())), preferred_element_type=f32)


def contract_first(first, second):
    return lax.dot_general(first, second, (((0,), (0,)), ((), ())), preferred_element_type=f32)


def adam_step(weight, grad, first, second, rate, decay):
    first = beta_one * first + (1.0 - beta_one) * grad
    second = beta_two * second + (1.0 - beta_two) * grad * grad
    corrected_first = first / (1.0 - beta_one**STEP)
    corrected_second = second / (1.0 - beta_two**STEP)
    fresh = weight - rate * (
        corrected_first / (jnp.sqrt(corrected_second) + adam_eps) + decay * weight
    )
    return (fresh, first, second)


def swiglu(gate_both, grad_act):
    rows, columns = gate_both.shape
    hidden = columns // 2
    block = 256

    def kernel(gate_ref, grad_ref, activation_out, grad_out):
        gate_part, up_part = gate_ref[:, :hidden], gate_ref[:, hidden:]
        grad = grad_ref[...]
        sigmoid = jax.nn.sigmoid(gate_part)
        gate_act = gate_part * sigmoid
        activation_out[...] = (gate_act * up_part).astype(bf16)
        grad_out[:, :hidden] = (
            grad * up_part * sigmoid * (1.0 + gate_part * (1.0 - sigmoid))
        ).astype(bf16)
        grad_out[:, hidden:] = (grad * gate_act).astype(bf16)

    def spec(width):
        return pl.BlockSpec((block, width), lambda step: (step, 0))

    return pl.pallas_call(
        kernel,
        grid=(rows // block,),
        in_specs=[spec(columns), spec(hidden)],
        out_specs=[spec(hidden), spec(columns)],
        out_shape=[
            jax.ShapeDtypeStruct((rows, hidden), bf16),
            jax.ShapeDtypeStruct((rows, columns), bf16),
        ],
        compiler_params=pltpu.CompilerParams(vmem_limit_bytes=40 * 2**20),
        cost_estimate=pl.CostEstimate(
            flops=20 * rows * hidden, bytes_accessed=18 * rows * hidden, transcendentals=rows * hidden
        ),
        name="swiglu",
    )(gate_both, grad_act)


def write_step(refs, grad, rate):
    weight_ref, first_ref, second_ref, grad_out, new_out, moment_out, square_out = refs
    fresh, first, second = adam_step(
        weight_ref[...], grad, first_ref[...], second_ref[...], rate, decay_rate
    )
    grad_out[...] = grad
    new_out[...] = fresh
    moment_out[...] = first
    square_out[...] = second


def gate_step(pieces, weight, first, second, rate, sharers, units):
    ranks, groups, rows, _ = pieces.shape
    block = pl.BlockSpec(
        (rows, sharers * ranks * units), lambda kind, group: (0, kind * groups + group)
    )

    def kernel(pieces_ref, *refs):
        parts = [pieces_ref[rank, 0].astype(f32) for rank in range(ranks)]
        grad = jnp.concatenate(
            [
                part[:, plane * units : (plane + 1) * units]
                for plane in range(sharers)
                for part in parts
            ],
            axis=1,
        )
        write_step(refs, grad, rate)

    return pl.pallas_call(
        kernel,
        grid=(2, groups),
        in_specs=[
            pl.BlockSpec(
                (ranks, 1, rows, sharers * units),
                lambda kind, group: (0, group, 0, kind),
            )
        ]
        + [block] * 3,
        out_specs=[block] * 4,
        out_shape=[jax.ShapeDtypeStruct(weight.shape, f32)] * 4,
        compiler_params=pltpu.CompilerParams(vmem_limit_bytes=40 * 2**20),
        cost_estimate=pl.CostEstimate(
            flops=20 * weight.size, bytes_accessed=30 * weight.size, transcendentals=weight.size
        ),
        name="gate_step",
    )(pieces, weight, first, second)


def attn_step(pieces, out_grad, weight, first, second, rate):
    ranks, rows, columns = pieces.shape
    local_width = columns // 3
    block = pl.BlockSpec((rows, ranks * local_width), lambda kind: (0, kind))

    def kernel(pieces_ref, out_ref, *refs):
        kind = pl.program_id(0)

        @pl.when(kind < 3)
        def _():
            parts = [pieces_ref[rank].astype(f32) for rank in range(ranks)]
            grad = jnp.concatenate(
                [
                    part[:, start : start + HEAD]
                    for start in range(0, local_width, HEAD)
                    for part in parts
                ],
                axis=1,
            )
            write_step(refs, grad, rate)

        @pl.when(kind == 3)
        def _():
            write_step(refs, out_ref[...], rate)

    return pl.pallas_call(
        kernel,
        grid=(4,),
        in_specs=[
            pl.BlockSpec((ranks, rows, local_width), lambda kind: (0, 0, jnp.minimum(kind, 2))),
            pl.BlockSpec((rows, ranks * local_width), lambda kind: (0, 0)),
        ]
        + [block] * 3,
        out_specs=[block] * 4,
        out_shape=[jax.ShapeDtypeStruct(weight.shape, f32)] * 4,
        compiler_params=pltpu.CompilerParams(vmem_limit_bytes=40 * 2**20),
        cost_estimate=pl.CostEstimate(
            flops=20 * weight.size, bytes_accessed=30 * weight.size, transcendentals=weight.size
        ),
        name="attn_step",
    )(pieces, out_grad, weight, first, second)


def first_half(shape):
    return lax.broadcasted_iota(jnp.int32, shape, 1) % HEAD < HEAD // 2


def of_head(values, head, axis=1):
    return jnp.where(
        lax.broadcasted_iota(jnp.int32, values.shape, axis) // HEAD == head,
        values,
        jnp.zeros_like(values),
    )


def rotate(values, cosine, sine):
    ahead = pltpu.roll(values, pair_width - HEAD // 2, 1)
    behind = pltpu.roll(values, HEAD // 2, 1)
    return values * cosine + jnp.where(first_half(values.shape), -ahead, behind) * sine


def unrotate(values, cosine, sine):
    sined = values * sine
    ahead = pltpu.roll(sined, pair_width - HEAD // 2, 1)
    behind = pltpu.roll(sined, HEAD // 2, 1)
    return values * cosine + jnp.where(first_half(values.shape), ahead, -behind)


def forward_kernel(
    query_ref,
    key_ref,
    value_ref,
    cos_rows,
    sin_rows,
    cos_ref,
    sin_ref,
    key_pos,
    query_pos,
    query_out,
    key_out,
    value_out,
    mixed_out,
    total_out,
):
    @pl.when(pl.program_id(1) == 0)
    def _():
        key_out[...] = rotate(key_ref[...], cos_ref[...], sin_ref[...]).astype(bf16)
        value_out[...] = value_ref[...].astype(bf16)

    queries = rotate(query_ref[...], cos_rows[...], sin_rows[...]).astype(bf16)
    query_out[...] = queries
    keys, values = key_out[...], value_out[...]
    allowed = key_pos[:, :1] <= query_pos[...]
    mixed = jnp.zeros((pair_width, queries.shape[0]), f32)
    for head in range(2):
        scores = contract_last(keys, of_head(queries, head) * bf16(score_scale))
        scores = jnp.where(allowed, scores, masked)
        peak = jnp.max(scores, axis=0, keepdims=True)
        weights = jnp.exp(scores - peak)
        total = jnp.sum(weights, axis=0, keepdims=True)
        probs = (weights * (1.0 / total)).astype(bf16)
        mixed += of_head(contract_first(values, probs), head, 0)
        total_out[head] = peak + jnp.log(total)
    mixed_out[...] = mixed.T.astype(bf16)


def backward_kernel(
    query_ref,
    key_ref,
    value_ref,
    grad_ref,
    total_ref,
    cos_rows,
    sin_rows,
    cos_ref,
    sin_ref,
    key_pos,
    query_pos,
    query_out,
    key_out,
    value_out,
    key_sum,
    value_sum,
):
    step = pl.program_id(1)

    @pl.when(step == 0)
    def _():
        key_sum[...] = jnp.zeros_like(key_sum)
        value_sum[...] = jnp.zeros_like(value_sum)

    keys, values = key_ref[...], value_ref[...]
    allowed = key_pos[:, :1] <= query_pos[...]
    grad_query = jnp.zeros((pair_width, query_ref.shape[0]), f32)
    for head in range(2):
        queries = of_head(query_ref[...], head) * bf16(score_scale)
        grads = of_head(grad_ref[...], head)
        scores = jnp.where(allowed, contract_last(keys, queries), masked)
        probs = jnp.exp(scores - total_ref[head])
        grad_probs = contract_last(values, grads)
        delta = jnp.sum(probs * grad_probs, axis=0, keepdims=True)
        grad_scores = (probs * (grad_probs - delta)).astype(bf16)
        value_sum[...] += dot(probs.astype(bf16), grads)
        key_sum[...] += dot(grad_scores, queries)
        grad_query += of_head(contract_first(keys, grad_scores), head, 0)
    query_out[...] = unrotate(
        (grad_query * score_scale).T, cos_rows[...], sin_rows[...]
    ).astype(bf16)

    @pl.when(step == pl.num_programs(1) - 1)
    def _():
        key_out[...] = unrotate(key_sum[...], cos_ref[...], sin_ref[...]).astype(bf16)
        value_out[...] = value_sum[...].astype(bf16)


def attention_specs(seq_len, pairs):
    rows = pl.BlockSpec((query_block, pair_width), lambda pair, step: (step, pair))
    whole = [
        pl.BlockSpec((seq_len, pair_width), lambda pair, step, at=at: (0, at * pairs + pair))
        for at in range(3)
    ]
    tables = [pl.BlockSpec((query_block, pair_width), lambda pair, step: (step, 0))] * 2 + [
        pl.BlockSpec((seq_len, pair_width), lambda pair, step: (0, 0))
    ] * 3
    places = pl.BlockSpec((1, query_block), lambda pair, step: (0, step))
    totals = pl.BlockSpec((2, 1, query_block), lambda pair, step: (pair, 0, step))
    return rows, whole, tables + [places], totals


def attention_forward(projected, tables):
    seq_len = projected.shape[0]
    pairs = projected.shape[1] // 3 // pair_width
    rows, whole, table_specs, totals = attention_specs(seq_len, pairs)
    low = jax.ShapeDtypeStruct((seq_len, pairs * pair_width), bf16)
    cosine, sine, key_pos, query_pos = tables
    return pl.pallas_call(
        forward_kernel,
        grid=(pairs, seq_len // query_block),
        in_specs=[rows, whole[1], whole[2]] + table_specs,
        out_specs=[rows, whole[0], whole[0], rows, totals],
        out_shape=[low] * 4 + [jax.ShapeDtypeStruct((2 * pairs, 1, seq_len), f32)],
        compiler_params=pltpu.CompilerParams(vmem_limit_bytes=40 * 2**20),
        cost_estimate=pl.CostEstimate(
            flops=pairs * seq_len * seq_len,
            bytes_accessed=seq_len * pairs * pair_width,
            transcendentals=0,
        ),
        name="attention_forward",
    )(projected, projected, projected, cosine, sine, cosine, sine, key_pos, query_pos)


def attention_backward(queries, keys, values, grads, totals, tables):
    seq_len = queries.shape[0]
    pairs = queries.shape[1] // pair_width
    rows, whole, table_specs, total_spec = attention_specs(seq_len, pairs)
    low = jax.ShapeDtypeStruct((seq_len, pairs * pair_width), bf16)
    cosine, sine, key_pos, query_pos = tables
    return pl.pallas_call(
        backward_kernel,
        grid=(pairs, seq_len // query_block),
        in_specs=[rows, whole[0], whole[0], rows, total_spec] + table_specs,
        out_specs=[rows, whole[0], whole[0]],
        out_shape=[low] * 3,
        scratch_shapes=[pltpu.VMEM((seq_len, pair_width), f32)] * 2,
        compiler_params=pltpu.CompilerParams(vmem_limit_bytes=40 * 2**20),
        cost_estimate=pl.CostEstimate(
            flops=pairs * seq_len * seq_len,
            bytes_accessed=seq_len * pairs * pair_width,
            transcendentals=0,
        ),
        name="attention_backward",
    )(queries, keys, values, grads, totals, cosine, sine, cosine, sine, key_pos, query_pos)


def swap(values, axis, bits):
    return lax.ppermute(values, axis, [(i, i ^ bits) for i in range(lax.axis_size(axis))])


def bit_of(axis, bit):
    return (lax.axis_index(axis) >> bit) & 1


def pick(values, index, axis):
    return lax.dynamic_index_in_dim(values, index, axis, keepdims=False)


def bit_count(axis):
    return lax.axis_size(axis).bit_length() - 1


def paired(values, axis, bit):
    other = swap(values, axis, 1 << bit)
    mine = bit_of(axis, bit) == 0
    return jnp.stack([jnp.where(mine, values, other), jnp.where(mine, other, values)])


def halved(values, axis, bit):
    values = values.reshape((2, values.shape[0] // 2) + values.shape[1:])
    own = bit_of(axis, bit)
    other = swap(pick(values, 1 - own, 0), axis, 1 << bit)
    return pick(values, own, 0).astype(f32) + other.astype(f32)


def after(values, *others):
    return lax.optimization_barrier((values, others))[0]


def row_orders():
    bits = list(range(1, bit_count("ctx")))
    return bits, bits[::-1]


def gather_even(own):
    orders = row_orders()
    parts = jnp.split(own, 2)
    for step in range(len(orders[0])):
        others = lax.optimization_barrier(
            [swap(part, "ctx", 1 << order[step]) for part, order in zip(parts, orders)]
        )
        merged = []
        for part, other, order in zip(parts, others, orders):
            low = bit_of("ctx", order[step]) == 0
            place = sum(bit > order[step] for bit in order[:step])
            merged.append(
                jnp.stack([jnp.where(low, part, other), jnp.where(low, other, part)], axis=place)
            )
        parts = merged
    return jnp.stack(parts, axis=len(orders[0]))


def gather_odd(even):
    other = swap(even, "ctx", 1)
    low = bit_of("ctx", 0) == 0
    whole = jnp.stack(
        [jnp.where(low, even, other), jnp.where(low, other, even)], axis=even.ndim - 3
    )
    return whole.reshape(-1, even.shape[-1])


def gather_whole(own):
    return lax.all_gather(own, "ctx", axis=0, tiled=True)


def scatter_rows(rows, weight, product, beside=None):
    ranks = lax.axis_size("ctx")
    own_rows = rows.shape[0] // ranks
    core = bit_of("ctx", 0)
    rows = rows.reshape(ranks // 2, 2, own_rows, rows.shape[1])

    def of_core(which):
        return pick(rows, which, 1).reshape(-1, rows.shape[-1])

    other = swap(product(of_core(1 - core), weight, 1 - core).astype(bf16), "ctx", 1)
    total = (product(of_core(core), weight, core) + other.astype(f32)).astype(bf16)
    orders = row_orders()
    count = len(orders[0])
    halves = total.reshape((2,) * count + (2, own_rows // 2, total.shape[-1]))
    parts = [lax.index_in_dim(halves, half, count, keepdims=False) for half in range(2)]
    for step in range(count)[::-1]:
        near, far = [], []
        for part, order in zip(parts, orders):
            place = sum(bit > order[step] for bit in order[:step])
            own = bit_of("ctx", order[step])
            near.append(pick(part, own, place))
            far.append(pick(part, 1 - own, place).astype(bf16))
        others = [swap(part, "ctx", 1 << order[step]) for part, order in zip(far, orders)]
        if step == 0:
            others, beside = lax.optimization_barrier((others, beside))
        else:
            others = lax.optimization_barrier(others)
        parts = [part.astype(f32) + other.astype(f32) for part, other in zip(near, others)]
    sums = jnp.concatenate(parts)
    return (sums, total) if beside is None else (sums, total, beside)


def exchange_held(pieces):
    pieces = lax.optimization_barrier(pieces)
    held = pieces[:1] + [
        swap(piece, "ctx", offset) for offset, piece in enumerate(pieces) if offset
    ]
    return lax.optimization_barrier(held)


def in_order(held, axis):
    held, me = jnp.stack(held), lax.axis_index("ctx")
    return jnp.stack([pick(held, me ^ rank, 0) for rank in range(held.shape[0])], axis=axis)


def exchange(pieces):
    me = lax.axis_index("ctx")
    return in_order(
        exchange_held([pick(pieces, me ^ offset, 0) for offset in range(pieces.shape[0])]), 0
    )


def body(
    tokens,
    cotangent,
    block_ids,
    attn_weight,
    gate_up,
    down_weight,
    norm_gains,
    attn_first,
    attn_second,
    gate_first,
    gate_second,
    down_first,
    down_second,
    gain_first,
    gain_second,
):
    every = ("dp", "ctx")
    width = attn_weight.shape[1] // 4
    planes = lax.axis_size("dp")
    ranks = lax.axis_size("ctx")
    own_rows = attn_weight.shape[0]
    units = down_weight.shape[0]
    rows = tokens.shape[1]
    half = rows // 2
    seq_len = rows * ranks
    local_heads = HEADS // ranks
    local_width = local_heads * HEAD
    aligned = local_heads == planes
    rank = lax.axis_index("ctx")
    top = bit_count("dp") - 1
    sharers = planes // 2
    side = bit_of("dp", top)
    hidden = sharers * units

    positions = (
        block_ids[:, None] * half + jnp.arange(half, dtype=jnp.int32)[None, :]
    ).reshape(-1)
    cosine, sine = angle_tables(positions)
    tables = (
        cosine,
        sine,
        jnp.broadcast_to(positions[:, None], (seq_len, pair_width)),
        positions[None, :],
    )

    gain_rows = 16
    inputs_even = gather_even(tokens[0])
    grad_out_theirs = swap(cotangent[0], "dp", 1 << top)

    attn_low = attn_weight.astype(bf16)
    qkv_pieces = (
        attn_low[:, : 3 * width]
        .reshape(own_rows, 3, local_heads, ranks, HEAD)
        .transpose(3, 0, 1, 2, 4)
        .reshape(ranks, own_rows, 3 * local_width)
    )
    qkv_own = exchange(qkv_pieces).reshape(ranks * own_rows, 3 * local_width)

    def over_planes(values):
        for bit in range(top):
            values = paired(values, "dp", bit)
        return values.reshape((sharers,) + values.shape[top:])

    gains_low = norm_gains.astype(bf16)
    for bit in range(bit_count("dp")):
        gains_low = paired(gains_low, "dp", bit)
    gains_own = gains_low.reshape(planes, 2 * own_rows)
    up_from = gate_up.shape[1] // 2
    gate_low = gate_up.astype(bf16)

    gain_piece = jnp.pad(
        gains_own, ((0, gain_rows - planes), (0, 2 * hidden - 2 * own_rows))
    )

    def rank_columns(at):
        return jnp.concatenate(
            [
                jnp.concatenate(
                    [
                        lax.dynamic_slice_in_dim(
                            gate_low, kind * up_from + (plane * ranks + at) * units, units, 1
                        )
                        for kind in range(2)
                        for plane in range(group * sharers, (group + 1) * sharers)
                    ],
                    axis=1,
                )
                for group in range(2)
            ]
            + [gain_piece]
        )

    gate_pieces = [rank_columns(rank ^ offset) for offset in range(ranks)]
    out_low = attn_low[:, 3 * width :]
    if aligned:
        out_proj = lax.all_gather(out_low, "dp", axis=0, tiled=True)
    else:
        out_all = lax.all_gather(out_low, every, axis=0, tiled=True)
        out_proj = pick(out_all.reshape(local_heads, ranks, HEAD, width), rank, 1)
        out_proj = out_proj.reshape(local_width, width)
    qkv_own, out_proj, gate_pieces = lax.optimization_barrier((qkv_own, out_proj, gate_pieces))
    qkv = lax.all_gather(qkv_own, "dp", axis=0, tiled=True)
    gate_pieces, inputs_even, grad_out_theirs = lax.optimization_barrier(
        (gate_pieces, inputs_even, grad_out_theirs)
    )
    gate_held = exchange_held(gate_pieces)
    gate_own = in_order([held[: 2 * own_rows].reshape(2, own_rows, -1) for held in gate_held], 1)
    gate_own = gate_own.reshape(2, ranks * own_rows, 2 * hidden)
    gains_low = in_order(
        [held[2 * own_rows : 2 * own_rows + planes, : 2 * own_rows] for held in gate_held], 0
    )
    gains_low = gains_low.reshape(ranks, planes, 2, own_rows).transpose(2, 1, 0, 3)
    gains_low = gains_low.reshape(2, width).astype(f32)
    gain_one, gain_two = gains_low[0], gains_low[1]
    inputs_low = gather_odd(inputs_even)
    inputs_all = inputs_low.astype(f32)
    normed_all = inputs_all * rms_scale(inputs_all)
    hidden_one = (normed_all * gain_one).astype(bf16)
    qkv, hidden_one, gate_own, gain_two, grad_out_own, grad_out_theirs, down = (
        lax.optimization_barrier(
            (
                qkv,
                hidden_one,
                gate_own,
                gain_two,
                cotangent[0],
                grad_out_theirs,
                down_weight.astype(bf16),
            )
        )
    )

    gate_mine = over_planes(pick(gate_own, side, 0))
    gate_halves = jnp.split(pick(gate_own, 1 - side, 0), 2)
    gate_halves[0] = swap(gate_halves[0], "dp", 1 << top)
    grad_out_near = gather_whole(grad_out_own)
    projected = dot(hidden_one, qkv)
    queries, keys, values, mixed_low, totals = attention_forward(projected, tables)
    mixed_low, gate_mine, gate_halves, down, grad_out_near, grad_out_theirs = (
        lax.optimization_barrier(
            (mixed_low, gate_mine, gate_halves, down, grad_out_near, grad_out_theirs)
        )
    )
    grad_out_far = gather_whole(grad_out_theirs)
    gate_halves[1] = swap(gate_halves[1], "dp", 1 << top)

    inputs = tokens[0].astype(f32)
    mixed_out, _, (gate_halves, grad_out_far) = scatter_rows(
        mixed_low, out_proj, dot, (gate_halves, grad_out_far)
    )
    gate_theirs = jnp.concatenate(gate_halves)
    middle = inputs + mixed_out
    inv_two = rms_scale(middle)
    normed_two = middle * inv_two
    hidden_two_own = (normed_two * gain_two).astype(bf16)
    hidden_two_near, hidden_two_theirs, gate_theirs, down = lax.optimization_barrier(
        (
            gather_whole(hidden_two_own),
            swap(hidden_two_own, "dp", 1 << top),
            over_planes(gate_theirs),
            down,
        ),
    )
    hidden_two_far = gather_whole(hidden_two_theirs)
    grad_outs = [grad_out_near, grad_out_far]
    down = over_planes(down).reshape(hidden, width)
    gate = jnp.concatenate(
        [
            jnp.where(side == 0, gate_mine, gate_theirs),
            jnp.where(side == 0, gate_theirs, gate_mine),
        ]
    ).reshape(width, 2 * hidden)

    def mlp(hidden_two, grad_out):
        return swiglu(dot(hidden_two, gate), contract_last(grad_out, down))

    activation_near, grad_both_near = mlp(hidden_two_near, grad_outs[0])
    grad_two, _ = scatter_rows(grad_both_near, gate, contract_last)
    hidden_two_far, grad_outs[1], grad_two = lax.optimization_barrier(
        (hidden_two_far, grad_outs[1], grad_two)
    )
    activation_far, grad_both_far = mlp(hidden_two_far, grad_outs[1])
    activations = [activation_near, activation_far]
    hidden_twos = [hidden_two_near, hidden_two_far]
    grad_boths = [grad_both_near, grad_both_far]

    def gate_terms(group):
        rows_in_group = width // 2
        terms = sum(
            contract_first(
                lax.dynamic_slice_in_dim(hidden_two, group * rows_in_group, rows_in_group, 1),
                grad_both,
            )
            for hidden_two, grad_both in zip(hidden_twos, grad_boths)
        )
        return terms.astype(bf16).reshape(sharers, ranks * own_rows, 2 * hidden)

    def sum_planes(values):
        for bit in range(top)[::-1]:
            values = halved(values.astype(bf16), "dp", bit)
        return values[0]

    grad_two_far, started = scatter_rows(grad_both_far, gate, contract_last)
    hidden_twos, grad_boths, activations, started = lax.optimization_barrier(
        (hidden_twos, grad_boths, activations, started)
    )
    term_theirs = sum_planes(gate_terms(1 - side)).astype(bf16)
    grad_two += swap(grad_two_far.astype(bf16), "dp", 1 << top).astype(f32)
    term_mine = gate_terms(side)
    down_term = sum(contract_first(a, g) for a, g in zip(activations, grad_outs)).astype(bf16)
    grad_two, term_mine, term_theirs, down_term, activations = lax.optimization_barrier(
        (grad_two, term_mine, term_theirs, down_term, activations)
    )
    theirs_halves = jnp.split(term_theirs, 2)
    theirs_halves[0] = swap(theirs_halves[0], "dp", 1 << top)
    output_far, _ = scatter_rows(activations[1], down, dot)
    down_grad = sum_planes(down_term.reshape(sharers, units, width))

    reduced_two = grad_two * gain_two
    grad_gain_two = jnp.sum(grad_two * normed_two, axis=0)
    grad_after = cotangent[0].astype(f32) + inv_two * (
        reduced_two - normed_two * jnp.mean(reduced_two * normed_two, axis=-1, keepdims=True)
    )
    after_low = gather_whole(grad_after.astype(bf16))
    grad_mixed = contract_last(after_low, out_proj).astype(bf16)
    out_term = contract_first(mixed_low, after_low).astype(bf16)
    grad_mixed, out_term, term_mine, theirs_halves, down_grad, output_far = (
        lax.optimization_barrier(
            (grad_mixed, out_term, term_mine, theirs_halves, down_grad, output_far)
        )
    )
    theirs_halves[1] = swap(theirs_halves[1], "dp", 1 << top)
    term_mine = sum_planes(term_mine).astype(bf16)
    grad_proj = jnp.concatenate(
        attention_backward(queries, keys, values, grad_mixed, totals, tables), axis=1
    )
    qkv_term = contract_first(hidden_one, grad_proj).astype(bf16)
    if aligned:
        out_term = out_term.reshape(width, local_width)
        qkv_term = jnp.concatenate([qkv_term, out_term], axis=1)
    else:
        spread = jnp.zeros((local_heads, ranks, HEAD, width), bf16)
        spread = lax.dynamic_update_index_in_dim(
            spread, out_term.reshape(local_heads, 1, HEAD, width), rank, 1
        )
        out_grad = lax.psum_scatter(
            spread.reshape(HEADS * HEAD, width), every, scatter_dimension=0, tiled=True
        )
    grad_proj, qkv_term, term_mine, theirs_halves = lax.optimization_barrier(
        (grad_proj, qkv_term, term_mine, theirs_halves)
    )
    term_theirs = jnp.concatenate(theirs_halves)
    qkv_term = lax.psum_scatter(qkv_term, "dp", scatter_dimension=0, tiled=True)
    if aligned:
        out_grad = qkv_term[:, 3 * local_width :].reshape(own_rows, width)
        qkv_term = qkv_term[:, : 3 * local_width]
    out_grad = out_grad.astype(f32)
    gain_one_parts = []

    def gained(part, weight, core):
        product = contract_last(part, weight)
        normed_part = pick(normed_all.reshape(ranks // 2, 2, rows, width), core, 1)
        gain_one_parts.append(jnp.sum(product * normed_part.reshape(-1, width), axis=0))
        return product

    grad_one, _ = scatter_rows(grad_proj, qkv, gained)
    grad_gain_one = sum(gain_one_parts)
    inv_one = rms_scale(inputs)
    normed_one = inputs * inv_one
    reduced_one = grad_one * gain_one
    grad_input = grad_after + inv_one * (
        reduced_one - normed_one * jnp.mean(reduced_one * normed_one, axis=-1, keepdims=True)
    )

    output_near, _ = scatter_rows(after(activations[0], grad_proj), down, dot)
    term_cols = jnp.stack(
        [
            jnp.where(side == 0, term_mine, term_theirs),
            jnp.where(side == 0, term_theirs, term_mine),
        ]
    )
    term_cols = term_cols.reshape(2, ranks, own_rows, 2 * hidden).transpose(1, 0, 2, 3)
    gate_pieces = exchange(term_cols)
    gain_grad = jnp.stack([grad_gain_one, grad_gain_two]).reshape(2, planes, ranks, -1)
    gain_grad = gain_grad.transpose(2, 1, 0, 3)
    for bit in range(bit_count("ctx"))[::-1]:
        gain_grad = halved(gain_grad, "ctx", bit)
    qkv_term, out_grad, gate_pieces, output_near, output_far, grad_input, gain_grad, down_grad = (
        lax.optimization_barrier(
            (
                qkv_term,
                out_grad,
                gate_pieces,
                output_near,
                output_far,
                grad_input,
                gain_grad,
                down_grad,
            )
        )
    )
    qkv_pieces = exchange(qkv_term.reshape(ranks, own_rows, 3 * local_width))
    output_far = swap(output_far.astype(bf16), "dp", 1 << top)
    gain_grad = gain_grad[0]
    for bit in range(bit_count("dp"))[::-1]:
        gain_grad = halved(gain_grad, "dp", bit)
    qkv_pieces, output_far, gain_grad = lax.optimization_barrier(
        (qkv_pieces, output_far, gain_grad)
    )
    outputs = middle + output_near + output_far.astype(f32)
    gain_grad = gain_grad.reshape(2, -1)
    attn_grad, attn_new, attn_moment, attn_square = attn_step(
        qkv_pieces, out_grad, attn_weight, attn_first, attn_second, 3.0 / math.sqrt(D)
    )
    gate_grad, gate_new, gate_moment, gate_square = gate_step(
        gate_pieces, gate_up, gate_first, gate_second, 3.0 / math.sqrt(D), sharers, units
    )
    down_new, down_moment, down_square = adam_step(
        down_weight, down_grad, down_first, down_second, 3.0 / math.sqrt(FF), decay_rate
    )
    gain_new, gain_moment, gain_square = adam_step(
        norm_gains, gain_grad, gain_first, gain_second, gain_rate, 0.0
    )
    return (
        outputs.astype(bf16)[None],
        grad_input.astype(bf16)[None],
        attn_grad,
        gate_grad,
        down_grad,
        gain_grad,
        attn_new,
        gate_new,
        down_new,
        gain_new,
        attn_moment,
        gate_moment,
        down_moment,
        gain_moment,
        attn_square,
        gate_square,
        down_square,
        gain_square,
    )


def solution(mesh):
    acts = P("dp", "ctx", None)
    weight = P(("dp", "ctx"), None)
    gains = P(None, ("dp", "ctx"))
    four = (weight, weight, weight, gains)
    return jax.shard_map(
        body,
        mesh=mesh,
        in_specs=(acts, acts, P()) + four + (weight,) * 6 + (gains,) * 2,
        out_specs=(acts, acts) + four * 4,
        check_vma=False,
    )
```

```python
import math

import jax
import jax.numpy as jnp
from jax import lax
from jax.experimental import pallas as pl
from jax.experimental.pallas import tpu as pltpu
from jax.sharding import PartitionSpec as P

D = 2048
HEADS = 32
HEAD = 64
FF = 8192
STEP = 5

norm_eps = 1e-05
rope_base = 130000.0
beta_one = 0.9
beta_two = 0.95
adam_eps = 1e-08
decay_rate = 0.1
gain_rate = 0.4
masked = -1e30
score_scale = HEAD ** (-0.5)
pair_width = 2 * HEAD
query_block = 256

bf16 = jnp.bfloat16
f32 = jnp.float32

light = pl.CostEstimate(flops=0, bytes_accessed=0, transcendentals=0)


def rms_scale(values):
    return lax.rsqrt(jnp.mean(values * values, axis=-1, keepdims=True) + norm_eps)


def angle_tables(positions):
    index = jnp.arange(HEAD // 2, dtype=f32)
    freqs = jnp.power(f32(rope_base), -2.0 * index / HEAD)
    phase = positions.astype(f32)[:, None] * freqs[None, :]
    return jnp.tile(jnp.cos(phase), (1, 4)), jnp.tile(jnp.sin(phase), (1, 4))


def dot(first, second, core=None):
    return jnp.dot(first, second, preferred_element_type=f32)


def contract_last(first, second, core=None):
    return lax.dot_general(first, second, (((1,), (1,)), ((), ())), preferred_element_type=f32)


def contract_first(first, second):
    return lax.dot_general(first, second, (((0,), (0,)), ((), ())), preferred_element_type=f32)


def thirds(values, axis):
    size = values.shape[axis] // 16
    first = -(-size // 3)
    second = first + (size - first + 1) // 2
    return jnp.split(values, [16 * first, 16 * second], axis=axis)


def adam_step(weight, grad, first, second, rate, decay):
    first = beta_one * first + (1.0 - beta_one) * grad
    second = beta_two * second + (1.0 - beta_two) * grad * grad
    corrected_first = first / (1.0 - beta_one**STEP)
    corrected_second = second / (1.0 - beta_two**STEP)
    fresh = weight - rate * (
        corrected_first / (jnp.sqrt(corrected_second) + adam_eps) + decay * weight
    )
    return (fresh, first, second)


def swiglu(gate_both, grad_act):
    rows, columns = gate_both.shape
    hidden = columns // 2
    block = 256

    def kernel(gate_ref, grad_ref, activation_out, grad_out):
        gate_part, up_part = gate_ref[:, :hidden], gate_ref[:, hidden:]
        grad = grad_ref[...]
        sigmoid = jax.nn.sigmoid(gate_part)
        gate_act = gate_part * sigmoid
        activation_out[...] = (gate_act * up_part).astype(bf16)
        grad_out[:, :hidden] = (
            grad * up_part * sigmoid * (1.0 + gate_part * (1.0 - sigmoid))
        ).astype(bf16)
        grad_out[:, hidden:] = (grad * gate_act).astype(bf16)

    def spec(width):
        return pl.BlockSpec((block, width), lambda step: (step, 0))

    return pl.pallas_call(
        kernel,
        grid=(rows // block,),
        in_specs=[spec(columns), spec(hidden)],
        out_specs=[spec(hidden), spec(columns)],
        out_shape=[
            jax.ShapeDtypeStruct((rows, hidden), bf16),
            jax.ShapeDtypeStruct((rows, columns), bf16),
        ],
        compiler_params=pltpu.CompilerParams(vmem_limit_bytes=40 * 2**20),
        cost_estimate=light,
        name="swiglu",
    )(gate_both, grad_act)


def normed_rows(inputs, gain):
    rows, width = inputs.shape
    block = 256

    def kernel(inputs_ref, gain_ref, normed_out):
        values = inputs_ref[...].astype(f32)
        normed_out[...] = (values * rms_scale(values) * gain_ref[...]).astype(bf16)

    spec = pl.BlockSpec((block, width), lambda step: (step, 0))
    return pl.pallas_call(
        kernel,
        grid=(rows // block,),
        in_specs=[spec, pl.BlockSpec((1, width), lambda step: (0, 0))],
        out_specs=spec,
        out_shape=jax.ShapeDtypeStruct((rows, width), bf16),
        compiler_params=pltpu.CompilerParams(vmem_limit_bytes=40 * 2**20),
        cost_estimate=light,
        name="normed_rows",
    )(inputs, gain.reshape(1, width))


def place_pieces(held, rank, groups, rows):
    ranks, columns = len(held), held[0].shape[1]

    def kernel(rank_ref, *refs):
        out_ref = refs[ranks]
        for group in range(groups):
            for offset in range(ranks):
                piece = refs[offset][group * rows : (group + 1) * rows]
                out_ref[group, rank_ref[0] ^ offset] = piece

    return pl.pallas_call(
        kernel,
        in_specs=[pl.BlockSpec(memory_space=pltpu.SMEM)]
        + [pl.BlockSpec(memory_space=pltpu.VMEM)] * ranks,
        out_specs=pl.BlockSpec(memory_space=pltpu.VMEM),
        out_shape=jax.ShapeDtypeStruct((groups, ranks, rows, columns), held[0].dtype),
        compiler_params=pltpu.CompilerParams(vmem_limit_bytes=40 * 2**20),
        cost_estimate=light,
        name="place_pieces",
    )(rank.reshape(1), *held)


def write_step(refs, grad, rate):
    weight_ref, first_ref, second_ref, grad_out, new_out, moment_out, square_out = refs
    fresh, first, second = adam_step(
        weight_ref[...], grad, first_ref[...], second_ref[...], rate, decay_rate
    )
    grad_out[...] = grad
    new_out[...] = fresh
    moment_out[...] = first
    square_out[...] = second


def plain_step(grad, weight, first, second, rate):
    rows, width = weight.shape
    block = pl.BlockSpec((rows // 4, width), lambda step: (step, 0))

    def kernel(grad_ref, *refs):
        write_step(refs, grad_ref[...], rate)

    return pl.pallas_call(
        kernel,
        grid=(4,),
        in_specs=[block] * 4,
        out_specs=[block] * 4,
        out_shape=[jax.ShapeDtypeStruct(weight.shape, f32)] * 4,
        compiler_params=pltpu.CompilerParams(vmem_limit_bytes=40 * 2**20),
        cost_estimate=light,
        name="plain_step",
    )(grad, weight, first, second)


def gate_step(pieces, weight, first, second, rate, sharers, units):
    ranks, groups, rows, _ = pieces.shape
    block = pl.BlockSpec(
        (rows, sharers * ranks * units), lambda kind, group: (0, kind * groups + group)
    )

    def kernel(pieces_ref, *refs):
        parts = [pieces_ref[rank, 0].astype(f32) for rank in range(ranks)]
        grad = jnp.concatenate(
            [
                part[:, plane * units : (plane + 1) * units]
                for plane in range(sharers)
                for part in parts
            ],
            axis=1,
        )
        write_step(refs, grad, rate)

    return pl.pallas_call(
        kernel,
        grid=(2, groups),
        in_specs=[
            pl.BlockSpec(
                (ranks, 1, rows, sharers * units),
                lambda kind, group: (0, group, 0, kind),
            )
        ]
        + [block] * 3,
        out_specs=[block] * 4,
        out_shape=[jax.ShapeDtypeStruct(weight.shape, f32)] * 4,
        compiler_params=pltpu.CompilerParams(vmem_limit_bytes=40 * 2**20),
        cost_estimate=pl.CostEstimate(
            flops=2**14 * weight.size, bytes_accessed=30 * weight.size, transcendentals=0
        ),
        name="gate_step",
    )(pieces, weight, first, second)


def attn_step(pieces, out_grad, weight, first, second, rate):
    ranks, rows, columns = pieces.shape
    local_width = columns // 3
    block = pl.BlockSpec((rows, ranks * local_width), lambda kind: (0, kind))

    def kernel(pieces_ref, out_ref, *refs):
        kind = pl.program_id(0)

        @pl.when(kind < 3)
        def _():
            parts = [pieces_ref[rank].astype(f32) for rank in range(ranks)]
            grad = jnp.concatenate(
                [
                    part[:, start : start + HEAD]
                    for start in range(0, local_width, HEAD)
                    for part in parts
                ],
                axis=1,
            )
            write_step(refs, grad, rate)

        @pl.when(kind == 3)
        def _():
            write_step(refs, out_ref[...], rate)

    return pl.pallas_call(
        kernel,
        grid=(4,),
        in_specs=[
            pl.BlockSpec((ranks, rows, local_width), lambda kind: (0, 0, jnp.minimum(kind, 2))),
            pl.BlockSpec((rows, ranks * local_width), lambda kind: (0, 0)),
        ]
        + [block] * 3,
        out_specs=[block] * 4,
        out_shape=[jax.ShapeDtypeStruct(weight.shape, f32)] * 4,
        compiler_params=pltpu.CompilerParams(vmem_limit_bytes=40 * 2**20),
        cost_estimate=light,
        name="attn_step",
    )(pieces, out_grad, weight, first, second)


def first_half(shape):
    return lax.broadcasted_iota(jnp.int32, shape, 1) % HEAD < HEAD // 2


def of_head(values, head, axis=1):
    return jnp.where(
        lax.broadcasted_iota(jnp.int32, values.shape, axis) // HEAD == head,
        values,
        jnp.zeros_like(values),
    )


def rotate(values, cosine, sine):
    ahead = pltpu.roll(values, pair_width - HEAD // 2, 1)
    behind = pltpu.roll(values, HEAD // 2, 1)
    return values * cosine + jnp.where(first_half(values.shape), -ahead, behind) * sine


def unrotate(values, cosine, sine):
    sined = values * sine
    ahead = pltpu.roll(sined, pair_width - HEAD // 2, 1)
    behind = pltpu.roll(sined, HEAD // 2, 1)
    return values * cosine + jnp.where(first_half(values.shape), ahead, -behind)


def forward_kernel(
    query_ref,
    key_ref,
    value_ref,
    cos_rows,
    sin_rows,
    cos_ref,
    sin_ref,
    key_pos,
    query_pos,
    query_out,
    key_out,
    value_out,
    mixed_out,
    total_out,
):
    @pl.when(pl.program_id(1) == 0)
    def _():
        key_out[...] = rotate(key_ref[...], cos_ref[...], sin_ref[...]).astype(bf16)
        value_out[...] = value_ref[...].astype(bf16)

    queries = rotate(query_ref[...], cos_rows[...], sin_rows[...]).astype(bf16)
    query_out[...] = queries
    keys, values = key_out[...], value_out[...]
    allowed = key_pos[:, :1] <= query_pos[...]
    mixed = jnp.zeros((pair_width, queries.shape[0]), f32)
    for head in range(2):
        scores = contract_last(keys, of_head(queries, head) * bf16(score_scale))
        scores = jnp.where(allowed, scores, masked)
        peak = jnp.max(scores, axis=0, keepdims=True)
        weights = jnp.exp(scores - peak)
        total = jnp.sum(weights, axis=0, keepdims=True)
        probs = (weights * (1.0 / total)).astype(bf16)
        mixed += of_head(contract_first(values, probs), head, 0)
        total_out[head] = peak + jnp.log(total)
    mixed_out[...] = mixed.T.astype(bf16)


def backward_kernel(
    query_ref,
    key_ref,
    value_ref,
    grad_ref,
    total_ref,
    cos_rows,
    sin_rows,
    cos_ref,
    sin_ref,
    key_pos,
    query_pos,
    query_out,
    key_out,
    value_out,
    key_sum,
    value_sum,
):
    step = pl.program_id(1)

    @pl.when(step == 0)
    def _():
        key_sum[...] = jnp.zeros_like(key_sum)
        value_sum[...] = jnp.zeros_like(value_sum)

    keys, values = key_ref[...], value_ref[...]
    allowed = key_pos[:, :1] <= query_pos[...]
    grad_query = jnp.zeros((pair_width, query_ref.shape[0]), f32)
    for head in range(2):
        queries = of_head(query_ref[...], head) * bf16(score_scale)
        grads = of_head(grad_ref[...], head)
        scores = jnp.where(allowed, contract_last(keys, queries), masked)
        probs = jnp.exp(scores - total_ref[head])
        grad_probs = contract_last(values, grads)
        delta = jnp.sum(probs * grad_probs, axis=0, keepdims=True)
        grad_scores = (probs * (grad_probs - delta)).astype(bf16)
        value_sum[...] += dot(probs.astype(bf16), grads)
        key_sum[...] += dot(grad_scores, queries)
        grad_query += of_head(contract_first(keys, grad_scores), head, 0)
    query_out[...] = unrotate(
        (grad_query * score_scale).T, cos_rows[...], sin_rows[...]
    ).astype(bf16)

    @pl.when(step == pl.num_programs(1) - 1)
    def _():
        key_out[...] = unrotate(key_sum[...], cos_ref[...], sin_ref[...]).astype(bf16)
        value_out[...] = value_sum[...].astype(bf16)


def attention_specs(seq_len, pairs):
    rows = pl.BlockSpec((query_block, pair_width), lambda pair, step: (step, pair))
    whole = [
        pl.BlockSpec((seq_len, pair_width), lambda pair, step, at=at: (0, at * pairs + pair))
        for at in range(3)
    ]
    tables = [pl.BlockSpec((query_block, pair_width), lambda pair, step: (step, 0))] * 2 + [
        pl.BlockSpec((seq_len, pair_width), lambda pair, step: (0, 0))
    ] * 3
    places = pl.BlockSpec((1, query_block), lambda pair, step: (0, step))
    totals = pl.BlockSpec((2, 1, query_block), lambda pair, step: (pair, 0, step))
    return rows, whole, tables + [places], totals


def attention_forward(projected, tables):
    seq_len = projected.shape[0]
    pairs = projected.shape[1] // 3 // pair_width
    rows, whole, table_specs, totals = attention_specs(seq_len, pairs)
    low = jax.ShapeDtypeStruct((seq_len, pairs * pair_width), bf16)
    cosine, sine, key_pos, query_pos = tables
    return pl.pallas_call(
        forward_kernel,
        grid=(pairs, seq_len // query_block),
        in_specs=[rows, whole[1], whole[2]] + table_specs,
        out_specs=[rows, whole[0], whole[0], rows, totals],
        out_shape=[low] * 4 + [jax.ShapeDtypeStruct((2 * pairs, 1, seq_len), f32)],
        compiler_params=pltpu.CompilerParams(vmem_limit_bytes=40 * 2**20),
        cost_estimate=light,
        name="attention_forward",
    )(projected, projected, projected, cosine, sine, cosine, sine, key_pos, query_pos)


def attention_backward(queries, keys, values, grads, totals, tables):
    seq_len = queries.shape[0]
    pairs = queries.shape[1] // pair_width
    rows, whole, table_specs, total_spec = attention_specs(seq_len, pairs)
    low = jax.ShapeDtypeStruct((seq_len, pairs * pair_width), bf16)
    cosine, sine, key_pos, query_pos = tables
    return pl.pallas_call(
        backward_kernel,
        grid=(pairs, seq_len // query_block),
        in_specs=[rows, whole[0], whole[0], rows, total_spec] + table_specs,
        out_specs=[rows, whole[0], whole[0]],
        out_shape=[low] * 3,
        scratch_shapes=[pltpu.VMEM((seq_len, pair_width), f32)] * 2,
        compiler_params=pltpu.CompilerParams(vmem_limit_bytes=40 * 2**20),
        cost_estimate=light,
        name="attention_backward",
    )(queries, keys, values, grads, totals, cosine, sine, cosine, sine, key_pos, query_pos)


def swap(values, axis, bits):
    return lax.ppermute(values, axis, [(i, i ^ bits) for i in range(lax.axis_size(axis))])


def bit_of(axis, bit):
    return (lax.axis_index(axis) >> bit) & 1


def pick(values, index, axis):
    return lax.dynamic_index_in_dim(values, index, axis, keepdims=False)


def bit_count(axis):
    return lax.axis_size(axis).bit_length() - 1


def paired(values, axis, bit):
    other = swap(values, axis, 1 << bit)
    mine = bit_of(axis, bit) == 0
    return jnp.stack([jnp.where(mine, values, other), jnp.where(mine, other, values)])


def halved(values, axis, bit):
    values = values.reshape((2, values.shape[0] // 2) + values.shape[1:])
    own = bit_of(axis, bit)
    other = swap(pick(values, 1 - own, 0), axis, 1 << bit)
    return pick(values, own, 0).astype(f32) + other.astype(f32)


def after(values, *others):
    return lax.optimization_barrier((values, others))[0]


def row_orders():
    bits = list(range(1, bit_count("ctx")))
    return bits, bits[::-1]


def gather_step(parts, step, beside=None):
    orders = row_orders()
    others = [swap(part, "ctx", 1 << order[step]) for part, order in zip(parts, orders)]
    others, beside = lax.optimization_barrier((others, beside))
    merged = []
    for part, other, order in zip(parts, others, orders):
        low = bit_of("ctx", order[step]) == 0
        place = sum(bit > order[step] for bit in order[:step])
        merged.append(
            jnp.stack([jnp.where(low, part, other), jnp.where(low, other, part)], axis=place)
        )
    return merged, beside


def gather_odd(even):
    other = swap(even, "ctx", 1)
    low = bit_of("ctx", 0) == 0
    whole = jnp.stack(
        [jnp.where(low, even, other), jnp.where(low, other, even)], axis=even.ndim - 3
    )
    return whole.reshape(-1, even.shape[-1])


def gather_whole(own):
    return lax.all_gather(own, "ctx", axis=0, tiled=True)


def scatter_rows(rows, weight, product, beside=None, ahead=None, then=None):
    ranks = lax.axis_size("ctx")
    own_rows = rows.shape[0] // ranks
    core = bit_of("ctx", 0)
    rows = rows.reshape(ranks // 2, 2, own_rows, rows.shape[1])

    def of_core(which):
        return pick(rows, which, 1).reshape(-1, rows.shape[-1])

    other = swap(product(of_core(1 - core), weight, 1 - core).astype(bf16), "ctx", 1)
    total = (product(of_core(core), weight, core) + other.astype(f32)).astype(bf16)
    orders = row_orders()
    count = len(orders[0])
    halves = total.reshape((2,) * count + (2, own_rows // 2, total.shape[-1]))
    parts = [lax.index_in_dim(halves, half, count, keepdims=False) for half in range(2)]
    for step in range(count)[::-1]:
        near, far = [], []
        for part, order in zip(parts, orders):
            place = sum(bit > order[step] for bit in order[:step])
            own = bit_of("ctx", order[step])
            near.append(pick(part, own, place))
            far.append(pick(part, 1 - own, place).astype(bf16))
        others = [swap(part, "ctx", 1 << order[step]) for part, order in zip(far, orders)]
        if step == 0:
            others, beside = lax.optimization_barrier((others, beside))
        else:
            others, ahead = lax.optimization_barrier((others, ahead))
            beside = then(ahead) if then else beside
        parts = [part.astype(f32) + other.astype(f32) for part, other in zip(near, others)]
    sums = jnp.concatenate(parts)
    return sums, total, beside, ahead


def exchange_held(pieces, beside=None):
    pieces = lax.optimization_barrier(pieces)
    held = pieces[:1] + [
        swap(piece, "ctx", offset) for offset, piece in enumerate(pieces) if offset
    ]
    return lax.optimization_barrier((held, beside))


def in_order(held, axis):
    held, me = jnp.stack(held), lax.axis_index("ctx")
    return jnp.stack([pick(held, me ^ rank, 0) for rank in range(held.shape[0])], axis=axis)


def exchange(pieces, beside=None):
    me = lax.axis_index("ctx")
    pieces = [pick(pieces, me ^ offset, 0) for offset in range(pieces.shape[0])]
    shape = pieces[0].shape
    held, beside = exchange_held(pieces, beside)
    held = [piece.reshape(-1, shape[-1]) for piece in held]
    placed = place_pieces(held, me, 1, held[0].shape[0]).reshape((len(held),) + shape)
    return placed if beside is None else (placed, beside)


def body(
    tokens,
    cotangent,
    block_ids,
    attn_weight,
    gate_up,
    down_weight,
    norm_gains,
    attn_first,
    attn_second,
    gate_first,
    gate_second,
    down_first,
    down_second,
    gain_first,
    gain_second,
):
    every = ("dp", "ctx")
    width = attn_weight.shape[1] // 4
    planes = lax.axis_size("dp")
    ranks = lax.axis_size("ctx")
    own_rows = attn_weight.shape[0]
    units = down_weight.shape[0]
    rows = tokens.shape[1]
    half = rows // 2
    seq_len = rows * ranks
    local_heads = HEADS // ranks
    local_width = local_heads * HEAD
    aligned = local_heads == planes
    rank = lax.axis_index("ctx")
    top = bit_count("dp") - 1
    sharers = planes // 2
    side = bit_of("dp", top)
    hidden = sharers * units

    positions = (
        block_ids[:, None] * half + jnp.arange(half, dtype=jnp.int32)[None, :]
    ).reshape(-1)
    cosine, sine = angle_tables(positions)
    tables = (
        cosine,
        sine,
        jnp.broadcast_to(positions[:, None], (seq_len, pair_width)),
        positions[None, :],
    )

    gain_rows = 16
    grad_out_theirs = swap(cotangent[0], "dp", 1 << top)

    attn_low = attn_weight.astype(bf16)
    qkv_pieces = (
        attn_low[:, : 3 * width]
        .reshape(own_rows, 3, local_heads, ranks, HEAD)
        .transpose(3, 0, 1, 2, 4)
        .reshape(ranks, own_rows, 3 * local_width)
    )
    def cross_planes(values):
        for bit in range(top - 1):
            values = paired(values, "dp", bit)
        return values, swap(values, "dp", 1 << (top - 1))

    def join_planes(pair):
        values, other = pair
        low = bit_of("dp", top - 1) == 0
        joined = jnp.stack([jnp.where(low, values, other), jnp.where(low, other, values)])
        return joined.reshape((sharers,) + values.shape[top - 1 :])

    gains_low = norm_gains.astype(bf16)
    inputs_even = jnp.split(tokens[0], 2)
    steps = len(row_orders()[0])
    plane = lax.axis_index("dp")
    gains_low = [gains_low] + [swap(gains_low, "dp", offset) for offset in range(1, planes)]
    inputs_even, gains_low = gather_step(inputs_even, 0, gains_low)
    for step in range(1, steps - 1):
        inputs_even = gather_step(inputs_even, step)[0]
    gains_low = jnp.stack(gains_low)
    gains_own = jnp.stack([pick(gains_low, plane ^ at, 0) for at in range(planes)])
    gains_own = gains_own.reshape(planes, 2 * own_rows)
    qkv_held = exchange_held([pick(qkv_pieces, rank ^ offset, 0) for offset in range(ranks)])[0]
    inputs_even, qkv_held = gather_step(inputs_even, steps - 1, qkv_held)
    inputs_even = jnp.stack(inputs_even, axis=steps)
    qkv_own = place_pieces(qkv_held, rank, 1, own_rows).reshape(
        ranks * own_rows, 3 * local_width
    )
    up_from = gate_up.shape[1] // 2
    gate_low = gate_up.astype(bf16)

    gain_piece = jnp.pad(
        gains_own, ((0, gain_rows - planes), (0, 2 * hidden - 2 * own_rows))
    )

    def rank_columns(at):
        return jnp.concatenate(
            [
                jnp.concatenate(
                    [
                        lax.dynamic_slice_in_dim(
                            gate_low, kind * up_from + (plane * ranks + at) * units, units, 1
                        )
                        for kind in range(2)
                        for plane in range(group * sharers, (group + 1) * sharers)
                    ],
                    axis=1,
                )
                for group in range(2)
            ]
            + [gain_piece]
        )

    gate_pieces = [rank_columns(rank ^ offset) for offset in range(ranks)]
    out_low = attn_low[:, 3 * width :]
    if aligned:
        out_proj = lax.all_gather(out_low, "dp", axis=0, tiled=True)
    else:
        out_all = lax.all_gather(out_low, every, axis=0, tiled=True)
        out_proj = pick(out_all.reshape(local_heads, ranks, HEAD, width), rank, 1)
        out_proj = out_proj.reshape(local_width, width)
    qkv_own, out_proj, gate_pieces, inputs_even = lax.optimization_barrier(
        (qkv_own, out_proj, gate_pieces, inputs_even)
    )
    qkv = lax.all_gather(qkv_own, "dp", axis=0, tiled=True)
    gate_held, grad_out_theirs = exchange_held(gate_pieces, grad_out_theirs)
    gate_own = place_pieces(gate_held, rank, 2, own_rows).reshape(
        2, ranks * own_rows, 2 * hidden
    )
    gains_low = in_order(
        [held[2 * own_rows : 2 * own_rows + planes, : 2 * own_rows] for held in gate_held], 0
    )
    gains_low = gains_low.reshape(ranks, planes, 2, own_rows).transpose(2, 1, 0, 3)
    gains_low = gains_low.reshape(2, width).astype(f32)
    gain_one, gain_two = gains_low[0], gains_low[1]
    inputs_low = gather_odd(inputs_even)
    hidden_one = normed_rows(inputs_low, gain_one)
    qkv, hidden_one, gate_own, gain_two, grad_out_own, grad_out_theirs, down = (
        lax.optimization_barrier(
            (
                qkv,
                hidden_one,
                gate_own,
                gain_two,
                cotangent[0],
                grad_out_theirs,
                down_weight.astype(bf16),
            )
        )
    )

    gate_mine = cross_planes(pick(gate_own, side, 0))
    gate_halves = jnp.split(pick(gate_own, 1 - side, 0), 2)
    gate_halves[0] = swap(gate_halves[0], "dp", 1 << top)
    grad_out_near = gather_whole(grad_out_own)
    projected = dot(hidden_one, qkv)
    queries, keys, values, mixed_low, totals = attention_forward(projected, tables)
    mixed_low, gate_mine, gate_halves, down_halves, grad_out_near, grad_out_theirs = (
        lax.optimization_barrier(
            (
                mixed_low,
                gate_mine,
                gate_halves,
                jnp.split(down, 2),
                grad_out_near,
                grad_out_theirs,
            )
        )
    )
    grad_out_far = gather_whole(grad_out_theirs)
    gate_halves[0] = cross_planes(gate_halves[0])
    gate_halves[1] = swap(gate_halves[1], "dp", 1 << top)

    inputs = tokens[0].astype(f32)
    mixed_out, _, (gate_halves, down_halves, grad_out_far), _ = scatter_rows(
        mixed_low, out_proj, dot, (gate_halves, down_halves, grad_out_far)
    )
    middle = inputs + mixed_out
    inv_two = rms_scale(middle)
    normed_two = middle * inv_two
    hidden_two_own = (normed_two * gain_two).astype(bf16)
    gate_halves[1] = cross_planes(gate_halves[1])
    down_halves[0] = cross_planes(down_halves[0])
    hidden_two_near, hidden_two_theirs, gate_halves, down_halves = lax.optimization_barrier(
        (
            gather_whole(hidden_two_own),
            swap(hidden_two_own, "dp", 1 << top),
            gate_halves,
            down_halves,
        ),
    )
    down_halves[1] = cross_planes(down_halves[1])
    gate_mine = join_planes(gate_mine)
    gate_theirs = jnp.concatenate([join_planes(pair) for pair in gate_halves], axis=1)
    down = jnp.concatenate([join_planes(pair) for pair in down_halves], axis=1)
    down = down.reshape(hidden, width)
    hidden_two_far = gather_whole(hidden_two_theirs)
    grad_outs = [grad_out_near, grad_out_far]
    gate = jnp.concatenate(
        [
            jnp.where(side == 0, gate_mine, gate_theirs),
            jnp.where(side == 0, gate_theirs, gate_mine),
        ]
    ).reshape(width, 2 * hidden)

    activation_near, grad_both_near = swiglu(
        dot(hidden_two_near, gate), contract_last(grad_outs[0], down)
    )
    grad_two, _, _, far_inputs = scatter_rows(
        grad_both_near, gate, contract_last, ahead=(hidden_two_far, grad_outs[1])
    )
    hidden_two_far, grad_outs[1] = far_inputs
    gate_both, grad_two = lax.optimization_barrier((dot(hidden_two_far, gate), grad_two))
    activation_far, grad_both_far = swiglu(gate_both, contract_last(grad_outs[1], down))
    activations = [activation_near, activation_far]
    hidden_twos = [hidden_two_near, hidden_two_far]
    grad_boths = [grad_both_near, grad_both_far]

    def gate_terms(group):
        rows_in_group = width // 2
        terms = sum(
            contract_first(
                lax.dynamic_slice_in_dim(hidden_two, group * rows_in_group, rows_in_group, 1),
                grad_both,
            )
            for hidden_two, grad_both in zip(hidden_twos, grad_boths)
        )
        return terms.astype(bf16).reshape(sharers, ranks * own_rows, 2 * hidden)

    def sum_planes(values):
        for bit in range(top)[::-1]:
            values = halved(values.astype(bf16), "dp", bit)
        return values[0]

    grad_two_far, started, _, _ = scatter_rows(grad_both_far, gate, contract_last)
    hidden_twos, grad_boths, activations, started = lax.optimization_barrier(
        (hidden_twos, grad_boths, activations, started)
    )
    down_term = sum(contract_first(a, g) for a, g in zip(activations, grad_outs)).astype(bf16)
    term_theirs = sum_planes(gate_terms(1 - side)).astype(bf16)
    grad_two += swap(grad_two_far.astype(bf16), "dp", 1 << top).astype(f32)
    term_mine = gate_terms(side)
    grad_two, term_mine, term_theirs, down_term, activations = lax.optimization_barrier(
        (grad_two, term_mine, term_theirs, down_term, activations)
    )
    theirs_parts = thirds(term_theirs, 0)
    down_parts = thirds(down_term.reshape(sharers, units, width), 1)
    def cross(parts, at):
        theirs, downs = list(parts[0]), list(parts[1])
        theirs[at] = swap(theirs[at], "dp", 1 << top)
        downs[at] = sum_planes(downs[at])
        return theirs, downs

    reduced_two = grad_two * gain_two
    grad_gain_two = jnp.sum(grad_two * normed_two, axis=0)
    grad_after = cotangent[0].astype(f32) + inv_two * (
        reduced_two - normed_two * jnp.mean(reduced_two * normed_two, axis=-1, keepdims=True)
    )
    after_low = gather_whole(grad_after.astype(bf16))
    output_far, _, parts, _ = scatter_rows(
        activations[1],
        down,
        dot,
        ahead=cross((theirs_parts, down_parts), 0),
        then=lambda parts: cross(parts, 1),
    )
    grad_mixed = contract_last(after_low, out_proj).astype(bf16)
    out_term = contract_first(mixed_low, after_low).astype(bf16)
    if aligned:
        out_term = out_term.reshape(width, local_width)
    grad_mixed, out_term, term_mine, parts, output_far = lax.optimization_barrier(
        (grad_mixed, out_term, term_mine, parts, output_far)
    )
    parts = cross(parts, 2)
    term_mine = sum_planes(term_mine).astype(bf16)
    grad_parts = attention_backward(queries, keys, values, grad_mixed, totals, tables)
    grad_parts, term_mine, parts = lax.optimization_barrier((grad_parts, term_mine, parts))
    term_theirs = jnp.concatenate(parts[0])
    down_grad = jnp.concatenate(parts[1])
    grad_proj = jnp.concatenate(grad_parts, axis=1)
    qkv_term = contract_first(hidden_one, grad_proj).astype(bf16)
    if aligned:
        qkv_term = jnp.concatenate([qkv_term, out_term], axis=1)
    else:
        spread = jnp.zeros((local_heads, ranks, HEAD, width), bf16)
        spread = lax.dynamic_update_index_in_dim(
            spread, out_term.reshape(local_heads, 1, HEAD, width), rank, 1
        )
        out_grad = lax.psum_scatter(
            spread.reshape(HEADS * HEAD, width), every, scatter_dimension=0, tiled=True
        )
    grad_proj, qkv_term, inputs_low, activation_near = lax.optimization_barrier(
        (grad_proj, qkv_term, inputs_low, activations[0])
    )
    qkv_term = lax.psum_scatter(qkv_term, "dp", scatter_dimension=0, tiled=True)
    if aligned:
        out_grad = qkv_term[:, 3 * local_width :].reshape(own_rows, width)
        qkv_term = qkv_term[:, : 3 * local_width]
    out_grad = out_grad.astype(f32)
    inputs_all = inputs_low.astype(f32)
    normed_all = inputs_all * rms_scale(inputs_all)
    gain_one_parts = []

    def gained(part, weight, core):
        product = contract_last(part, weight)
        normed_part = pick(normed_all.reshape(ranks // 2, 2, rows, width), core, 1)
        gain_one_parts.append(jnp.sum(product * normed_part.reshape(-1, width), axis=0))
        return product

    grad_one = scatter_rows(grad_proj, qkv, gained)[0]
    grad_gain_one = sum(gain_one_parts)
    inv_one = rms_scale(inputs)
    normed_one = inputs * inv_one
    reduced_one = grad_one * gain_one
    grad_input = grad_after + inv_one * (
        reduced_one - normed_one * jnp.mean(reduced_one * normed_one, axis=-1, keepdims=True)
    )

    output_near = scatter_rows(activation_near, down, dot)[0]
    term_cols = jnp.stack(
        [
            jnp.where(side == 0, term_mine, term_theirs),
            jnp.where(side == 0, term_theirs, term_mine),
        ]
    )
    term_cols = term_cols.reshape(2, ranks, own_rows, 2 * hidden).transpose(1, 0, 2, 3)
    gate_pieces = exchange(term_cols)
    gain_grad = jnp.stack([grad_gain_one, grad_gain_two]).reshape(2, planes, ranks, -1)
    gain_grad = gain_grad.transpose(2, 1, 0, 3)
    for bit in range(bit_count("ctx"))[::-1]:
        gain_grad = halved(gain_grad, "ctx", bit)
    gate_stepped = gate_step(
        gate_pieces, gate_up, gate_first, gate_second, 3.0 / math.sqrt(D), sharers, units
    )
    down_stepped = plain_step(
        down_grad, down_weight, down_first, down_second, 3.0 / math.sqrt(FF)
    )
    held_back = (gate_stepped, down_stepped, output_near, output_far, grad_input, gain_grad)
    qkv_term, out_grad, held_back = lax.optimization_barrier((qkv_term, out_grad, held_back))
    gate_stepped, down_stepped, output_near, output_far, grad_input, gain_grad = held_back
    gate_grad, gate_new, gate_moment, gate_square = gate_stepped
    down_grad, down_new, down_moment, down_square = down_stepped
    output_far = output_far.astype(bf16)
    gain_parts = [pick(gain_grad[0], plane ^ offset, 0) for offset in range(planes)]
    qkv_pieces, output_far = exchange(
        qkv_term.reshape(ranks, own_rows, 3 * local_width), swap(output_far, "dp", 1 << top)
    )
    gain_parts, output_far = lax.optimization_barrier((gain_parts, output_far))
    outputs = middle + output_near + output_far.astype(f32)
    gain_grad = sum(
        gain_parts[:1]
        + [swap(part, "dp", offset) for offset, part in enumerate(gain_parts) if offset]
    )
    gain_grad = gain_grad.reshape(2, -1)
    attn_grad, attn_new, attn_moment, attn_square = attn_step(
        qkv_pieces, out_grad, attn_weight, attn_first, attn_second, 3.0 / math.sqrt(D)
    )
    gain_new, gain_moment, gain_square = adam_step(
        norm_gains, gain_grad, gain_first, gain_second, gain_rate, 0.0
    )
    return (
        outputs.astype(bf16)[None],
        grad_input.astype(bf16)[None],
        attn_grad,
        gate_grad,
        down_grad,
        gain_grad,
        attn_new,
        gate_new,
        down_new,
        gain_new,
        attn_moment,
        gate_moment,
        down_moment,
        gain_moment,
        attn_square,
        gate_square,
        down_square,
        gain_square,
    )


def solution(mesh):
    acts = P("dp", "ctx", None)
    weight = P(("dp", "ctx"), None)
    gains = P(None, ("dp", "ctx"))
    four = (weight, weight, weight, gains)
    return jax.shard_map(
        body,
        mesh=mesh,
        in_specs=(acts, acts, P()) + four + (weight,) * 6 + (gains,) * 2,
        out_specs=(acts, acts) + four * 4,
        check_vma=False,
    )
```

```python
import math

import jax
import jax.numpy as jnp
from jax import lax
from jax.experimental import pallas as pl
from jax.experimental.pallas import tpu as pltpu
from jax.sharding import PartitionSpec as P

D = 2048
HEADS = 32
HEAD = 64
FF = 8192
STEP = 5

norm_eps = 1e-05
rope_base = 130000.0
beta_one = 0.9
beta_two = 0.95
adam_eps = 1e-08
decay_rate = 0.1
gain_rate = 0.4
masked = -1e30
score_scale = HEAD ** (-0.5)
pair_width = 2 * HEAD
query_block = 256

bf16 = jnp.bfloat16
f32 = jnp.float32

light = pl.CostEstimate(flops=0, bytes_accessed=0, transcendentals=0)


def rms_scale(values):
    return lax.rsqrt(jnp.mean(values * values, axis=-1, keepdims=True) + norm_eps)


def angle_tables(positions):
    index = jnp.arange(HEAD // 2, dtype=f32)
    freqs = jnp.power(f32(rope_base), -2.0 * index / HEAD)
    phase = positions.astype(f32)[:, None] * freqs[None, :]
    return jnp.tile(jnp.cos(phase), (1, 4)), jnp.tile(jnp.sin(phase), (1, 4))


def dot(first, second):
    return jnp.dot(first, second, preferred_element_type=f32)


def contract_last(first, second):
    return lax.dot_general(first, second, (((1,), (1,)), ((), ())), preferred_element_type=f32)


def contract_first(first, second):
    return lax.dot_general(first, second, (((0,), (0,)), ((), ())), preferred_element_type=f32)


def thirds(values, axis):
    size = values.shape[axis] // 16
    first = -(-size // 3)
    second = first + (size - first + 1) // 2
    return jnp.split(values, [16 * first, 16 * second], axis=axis)


def adam_step(weight, grad, first, second, rate, decay):
    first = beta_one * first + (1.0 - beta_one) * grad
    second = beta_two * second + (1.0 - beta_two) * grad * grad
    corrected_first = first / (1.0 - beta_one**STEP)
    corrected_second = second / (1.0 - beta_two**STEP)
    fresh = weight - rate * (
        corrected_first / (jnp.sqrt(corrected_second) + adam_eps) + decay * weight
    )
    return (fresh, first, second)


def swiglu(gate_both, grad_act):
    rows, columns = gate_both.shape
    hidden = columns // 2
    block = 256

    def kernel(gate_ref, grad_ref, activation_out, grad_out):
        gate_part, up_part = gate_ref[:, :hidden], gate_ref[:, hidden:]
        grad = grad_ref[...]
        sigmoid = jax.nn.sigmoid(gate_part)
        gate_act = gate_part * sigmoid
        activation_out[...] = (gate_act * up_part).astype(bf16)
        grad_out[:, :hidden] = (
            grad * up_part * sigmoid * (1.0 + gate_part * (1.0 - sigmoid))
        ).astype(bf16)
        grad_out[:, hidden:] = (grad * gate_act).astype(bf16)

    def spec(width):
        return pl.BlockSpec((block, width), lambda step: (step, 0))

    return pl.pallas_call(
        kernel,
        grid=(rows // block,),
        in_specs=[spec(columns), spec(hidden)],
        out_specs=[spec(hidden), spec(columns)],
        out_shape=[
            jax.ShapeDtypeStruct((rows, hidden), bf16),
            jax.ShapeDtypeStruct((rows, columns), bf16),
        ],
        compiler_params=pltpu.CompilerParams(vmem_limit_bytes=40 * 2**20),
        cost_estimate=light,
        name="swiglu",
    )(gate_both, grad_act)


def normed_rows(inputs, gain):
    rows, width = inputs.shape
    block = 256

    def kernel(inputs_ref, gain_ref, normed_out, scale_out):
        values = inputs_ref[...].astype(f32)
        scale = rms_scale(values)
        normed_out[...] = (values * scale * gain_ref[...]).astype(bf16)
        scale_out[...] = jnp.broadcast_to(scale, scale_out.shape)

    spec = pl.BlockSpec((block, width), lambda step: (step, 0))
    return pl.pallas_call(
        kernel,
        grid=(rows // block,),
        in_specs=[spec, pl.BlockSpec((1, width), lambda step: (0, 0))],
        out_specs=[spec, pl.BlockSpec((block, 128), lambda step: (step, 0))],
        out_shape=[
            jax.ShapeDtypeStruct((rows, width), bf16),
            jax.ShapeDtypeStruct((rows, 128), f32),
        ],
        compiler_params=pltpu.CompilerParams(vmem_limit_bytes=40 * 2**20),
        cost_estimate=light,
        name="normed_rows",
    )(inputs, gain.reshape(1, width))


def place_pieces(held, rank, groups, rows):
    ranks, columns = len(held), held[0].shape[1]

    def kernel(rank_ref, *refs):
        out_ref = refs[ranks]
        for group in range(groups):
            for offset in range(ranks):
                piece = refs[offset][group * rows : (group + 1) * rows]
                out_ref[group, rank_ref[0] ^ offset] = piece

    return pl.pallas_call(
        kernel,
        in_specs=[pl.BlockSpec(memory_space=pltpu.SMEM)]
        + [pl.BlockSpec(memory_space=pltpu.VMEM)] * ranks,
        out_specs=pl.BlockSpec(memory_space=pltpu.VMEM),
        out_shape=jax.ShapeDtypeStruct((groups, ranks, rows, columns), held[0].dtype),
        compiler_params=pltpu.CompilerParams(vmem_limit_bytes=40 * 2**20),
        cost_estimate=light,
        name="place_pieces",
    )(rank.reshape(1), *held)


def core_product(rows, weight, core, other, transposed, normed=None):
    groups, _, own_rows, depth = rows.shape
    width = weight.shape[0] if transposed else weight.shape[1]
    count, block = groups * own_rows, 512

    def kernel(core_ref, rows_ref, weight_ref, *refs):
        refs = list(refs)
        part = rows_ref[...].reshape(count, depth)
        contract = ((1,), (1,)) if transposed else ((1,), (0,))
        product = lax.dot_general(
            part, weight_ref[...], (contract, ((), ())), preferred_element_type=f32
        )
        if normed is not None:
            inputs_ref, scale_ref, gain_out = refs.pop(0), refs.pop(0), refs.pop()
            values = inputs_ref[...].reshape(count, block).astype(f32)
            scale = scale_ref[...].reshape(count, 128)[:, :1]
            gain_out[...] = jnp.sum(product * (values * scale), axis=0, keepdims=True)
        if other is not None:
            product += refs.pop(0)[...].astype(f32)
        refs[0][...] = product.astype(bf16)

    def of_core(columns, moving):
        return pl.BlockSpec(
            (groups, 1, own_rows, columns),
            lambda step, core_ref: (0, core_ref[0], 0, step if moving else 0),
        )

    operands = [rows, weight]
    in_specs = [
        of_core(depth, False),
        pl.BlockSpec((block, depth), lambda step, core_ref: (step, 0))
        if transposed
        else pl.BlockSpec((depth, block), lambda step, core_ref: (0, step)),
    ]
    column = pl.BlockSpec((count, block), lambda step, core_ref: (0, step))
    out_specs, out_shape = [column], [jax.ShapeDtypeStruct((count, width), bf16)]
    if normed is not None:
        operands += [values.reshape(groups, 2, own_rows, -1) for values in normed]
        in_specs += [of_core(block, True), of_core(128, False)]
        out_specs.append(pl.BlockSpec((1, block), lambda step, core_ref: (0, step)))
        out_shape.append(jax.ShapeDtypeStruct((1, width), f32))
    if other is not None:
        operands.append(other)
        in_specs.append(column)
    return pl.pallas_call(
        kernel,
        grid_spec=pltpu.PrefetchScalarGridSpec(
            num_scalar_prefetch=1,
            grid=(width // block,),
            in_specs=in_specs,
            out_specs=out_specs,
        ),
        out_shape=out_shape,
        compiler_params=pltpu.CompilerParams(vmem_limit_bytes=40 * 2**20),
        cost_estimate=light,
        name="core_product",
    )(core.reshape(1), *operands)


def write_step(refs, grad, rate):
    weight_ref, first_ref, second_ref, grad_out, new_out, moment_out, square_out = refs
    fresh, first, second = adam_step(
        weight_ref[...], grad, first_ref[...], second_ref[...], rate, decay_rate
    )
    grad_out[...] = grad
    new_out[...] = fresh
    moment_out[...] = first
    square_out[...] = second


def plain_step(grad, weight, first, second, rate):
    rows, width = weight.shape
    block = pl.BlockSpec((rows // 4, width), lambda step: (step, 0))

    def kernel(grad_ref, *refs):
        write_step(refs, grad_ref[...], rate)

    return pl.pallas_call(
        kernel,
        grid=(4,),
        in_specs=[block] * 4,
        out_specs=[block] * 4,
        out_shape=[jax.ShapeDtypeStruct(weight.shape, f32)] * 4,
        compiler_params=pltpu.CompilerParams(vmem_limit_bytes=40 * 2**20),
        cost_estimate=light,
        name="plain_step",
    )(grad, weight, first, second)


def gate_step(pieces, weight, first, second, rate, sharers, units):
    ranks, groups, rows, _ = pieces.shape
    block = pl.BlockSpec(
        (rows, sharers * ranks * units), lambda kind, group: (0, kind * groups + group)
    )

    def kernel(pieces_ref, *refs):
        parts = [pieces_ref[rank, 0].astype(f32) for rank in range(ranks)]
        grad = jnp.concatenate(
            [
                part[:, plane * units : (plane + 1) * units]
                for plane in range(sharers)
                for part in parts
            ],
            axis=1,
        )
        write_step(refs, grad, rate)

    return pl.pallas_call(
        kernel,
        grid=(2, groups),
        in_specs=[
            pl.BlockSpec(
                (ranks, 1, rows, sharers * units),
                lambda kind, group: (0, group, 0, kind),
            )
        ]
        + [block] * 3,
        out_specs=[block] * 4,
        out_shape=[jax.ShapeDtypeStruct(weight.shape, f32)] * 4,
        compiler_params=pltpu.CompilerParams(vmem_limit_bytes=40 * 2**20),
        cost_estimate=pl.CostEstimate(
            flops=2**12 * weight.size, bytes_accessed=weight.size, transcendentals=0
        ),
        name="gate_step",
    )(pieces, weight, first, second)


def attn_step(pieces, out_grad, weight, first, second, rate):
    ranks, rows, columns = pieces.shape
    local_width = columns // 3
    block = pl.BlockSpec((rows, ranks * local_width), lambda kind: (0, kind))

    def kernel(pieces_ref, out_ref, *refs):
        kind = pl.program_id(0)

        @pl.when(kind < 3)
        def _():
            parts = [pieces_ref[rank].astype(f32) for rank in range(ranks)]
            grad = jnp.concatenate(
                [
                    part[:, start : start + HEAD]
                    for start in range(0, local_width, HEAD)
                    for part in parts
                ],
                axis=1,
            )
            write_step(refs, grad, rate)

        @pl.when(kind == 3)
        def _():
            write_step(refs, out_ref[...], rate)

    return pl.pallas_call(
        kernel,
        grid=(4,),
        in_specs=[
            pl.BlockSpec((ranks, rows, local_width), lambda kind: (0, 0, jnp.minimum(kind, 2))),
            pl.BlockSpec((rows, ranks * local_width), lambda kind: (0, 0)),
        ]
        + [block] * 3,
        out_specs=[block] * 4,
        out_shape=[jax.ShapeDtypeStruct(weight.shape, f32)] * 4,
        compiler_params=pltpu.CompilerParams(vmem_limit_bytes=40 * 2**20),
        cost_estimate=light,
        name="attn_step",
    )(pieces, out_grad, weight, first, second)


def first_half(shape):
    return lax.broadcasted_iota(jnp.int32, shape, 1) % HEAD < HEAD // 2


def of_head(values, head, axis=1):
    return jnp.where(
        lax.broadcasted_iota(jnp.int32, values.shape, axis) // HEAD == head,
        values,
        jnp.zeros_like(values),
    )


def rotate(values, cosine, sine):
    ahead = pltpu.roll(values, pair_width - HEAD // 2, 1)
    behind = pltpu.roll(values, HEAD // 2, 1)
    return values * cosine + jnp.where(first_half(values.shape), -ahead, behind) * sine


def unrotate(values, cosine, sine):
    sined = values * sine
    ahead = pltpu.roll(sined, pair_width - HEAD // 2, 1)
    behind = pltpu.roll(sined, HEAD // 2, 1)
    return values * cosine + jnp.where(first_half(values.shape), ahead, -behind)


def forward_kernel(
    query_ref,
    key_ref,
    value_ref,
    cos_rows,
    sin_rows,
    cos_ref,
    sin_ref,
    key_pos,
    query_pos,
    query_out,
    key_out,
    value_out,
    mixed_out,
    total_out,
):
    @pl.when(pl.program_id(1) == 0)
    def _():
        key_out[...] = rotate(key_ref[...], cos_ref[...], sin_ref[...]).astype(bf16)
        value_out[...] = value_ref[...].astype(bf16)

    queries = rotate(query_ref[...], cos_rows[...], sin_rows[...]).astype(bf16)
    query_out[...] = queries
    keys, values = key_out[...], value_out[...]
    allowed = key_pos[:, :1] <= query_pos[...]
    mixed = jnp.zeros((pair_width, queries.shape[0]), f32)
    for head in range(2):
        scores = contract_last(keys, of_head(queries, head) * bf16(score_scale))
        scores = jnp.where(allowed, scores, masked)
        peak = jnp.max(scores, axis=0, keepdims=True)
        weights = jnp.exp(scores - peak)
        total = jnp.sum(weights, axis=0, keepdims=True)
        probs = (weights * (1.0 / total)).astype(bf16)
        mixed += of_head(contract_first(values, probs), head, 0)
        total_out[head] = peak + jnp.log(total)
    mixed_out[...] = mixed.T.astype(bf16)


def backward_kernel(
    query_ref,
    key_ref,
    value_ref,
    grad_ref,
    total_ref,
    cos_rows,
    sin_rows,
    cos_ref,
    sin_ref,
    key_pos,
    query_pos,
    query_out,
    key_out,
    value_out,
    key_sum,
    value_sum,
):
    step = pl.program_id(1)

    @pl.when(step == 0)
    def _():
        key_sum[...] = jnp.zeros_like(key_sum)
        value_sum[...] = jnp.zeros_like(value_sum)

    keys, values = key_ref[...], value_ref[...]
    allowed = key_pos[:, :1] <= query_pos[...]
    grad_query = jnp.zeros((pair_width, query_ref.shape[0]), f32)
    for head in range(2):
        queries = of_head(query_ref[...], head) * bf16(score_scale)
        grads = of_head(grad_ref[...], head)
        scores = jnp.where(allowed, contract_last(keys, queries), masked)
        probs = jnp.exp(scores - total_ref[head])
        grad_probs = contract_last(values, grads)
        delta = jnp.sum(probs * grad_probs, axis=0, keepdims=True)
        grad_scores = (probs * (grad_probs - delta)).astype(bf16)
        value_sum[...] += dot(probs.astype(bf16), grads)
        key_sum[...] += dot(grad_scores, queries)
        grad_query += of_head(contract_first(keys, grad_scores), head, 0)
    query_out[...] = unrotate(
        (grad_query * score_scale).T, cos_rows[...], sin_rows[...]
    ).astype(bf16)

    @pl.when(step == pl.num_programs(1) - 1)
    def _():
        key_out[...] = unrotate(key_sum[...], cos_ref[...], sin_ref[...]).astype(bf16)
        value_out[...] = value_sum[...].astype(bf16)


def attention_specs(seq_len, pairs):
    rows = pl.BlockSpec((query_block, pair_width), lambda pair, step: (step, pair))
    whole = [
        pl.BlockSpec((seq_len, pair_width), lambda pair, step, at=at: (0, at * pairs + pair))
        for at in range(3)
    ]
    tables = [pl.BlockSpec((query_block, pair_width), lambda pair, step: (step, 0))] * 2 + [
        pl.BlockSpec((seq_len, pair_width), lambda pair, step: (0, 0))
    ] * 3
    places = pl.BlockSpec((1, query_block), lambda pair, step: (0, step))
    totals = pl.BlockSpec((2, 1, query_block), lambda pair, step: (pair, 0, step))
    return rows, whole, tables + [places], totals


def attention_forward(projected, tables):
    seq_len = projected.shape[0]
    pairs = projected.shape[1] // 3 // pair_width
    rows, whole, table_specs, totals = attention_specs(seq_len, pairs)
    low = jax.ShapeDtypeStruct((seq_len, pairs * pair_width), bf16)
    cosine, sine, key_pos, query_pos = tables
    return pl.pallas_call(
        forward_kernel,
        grid=(pairs, seq_len // query_block),
        in_specs=[rows, whole[1], whole[2]] + table_specs,
        out_specs=[rows, whole[0], whole[0], rows, totals],
        out_shape=[low] * 4 + [jax.ShapeDtypeStruct((2 * pairs, 1, seq_len), f32)],
        compiler_params=pltpu.CompilerParams(vmem_limit_bytes=40 * 2**20),
        cost_estimate=light,
        name="attention_forward",
    )(projected, projected, projected, cosine, sine, cosine, sine, key_pos, query_pos)


def attention_backward(queries, keys, values, grads, totals, tables):
    seq_len = queries.shape[0]
    pairs = queries.shape[1] // pair_width
    rows, whole, table_specs, total_spec = attention_specs(seq_len, pairs)
    low = jax.ShapeDtypeStruct((seq_len, pairs * pair_width), bf16)
    cosine, sine, key_pos, query_pos = tables
    return pl.pallas_call(
        backward_kernel,
        grid=(pairs, seq_len // query_block),
        in_specs=[rows, whole[0], whole[0], rows, total_spec] + table_specs,
        out_specs=[rows, whole[0], whole[0]],
        out_shape=[low] * 3,
        scratch_shapes=[pltpu.VMEM((seq_len, pair_width), f32)] * 2,
        compiler_params=pltpu.CompilerParams(vmem_limit_bytes=40 * 2**20),
        cost_estimate=light,
        name="attention_backward",
    )(queries, keys, values, grads, totals, cosine, sine, cosine, sine, key_pos, query_pos)


def swap(values, axis, bits):
    return lax.ppermute(values, axis, [(i, i ^ bits) for i in range(lax.axis_size(axis))])


def bit_of(axis, bit):
    return (lax.axis_index(axis) >> bit) & 1


def pick(values, index, axis):
    return lax.dynamic_index_in_dim(values, index, axis, keepdims=False)


def bit_count(axis):
    return lax.axis_size(axis).bit_length() - 1


def paired(values, axis, bit):
    other = swap(values, axis, 1 << bit)
    mine = bit_of(axis, bit) == 0
    return jnp.stack([jnp.where(mine, values, other), jnp.where(mine, other, values)])


def halved(values, axis, bit):
    values = values.reshape((2, values.shape[0] // 2) + values.shape[1:])
    own = bit_of(axis, bit)
    other = swap(pick(values, 1 - own, 0), axis, 1 << bit)
    return pick(values, own, 0).astype(f32) + other.astype(f32)


def after(values, *others):
    return lax.optimization_barrier((values, others))[0]


def row_orders():
    bits = list(range(1, bit_count("ctx")))
    return bits, bits[::-1]


def gather_step(parts, step, beside=None):
    orders = row_orders()
    others = [swap(part, "ctx", 1 << order[step]) for part, order in zip(parts, orders)]
    others, beside = lax.optimization_barrier((others, beside))
    merged = []
    for part, other, order in zip(parts, others, orders):
        low = bit_of("ctx", order[step]) == 0
        place = sum(bit > order[step] for bit in order[:step])
        merged.append(
            jnp.stack([jnp.where(low, part, other), jnp.where(low, other, part)], axis=place)
        )
    return merged, beside


def gather_odd(even):
    other = swap(even, "ctx", 1)
    low = bit_of("ctx", 0) == 0
    whole = jnp.stack(
        [jnp.where(low, even, other), jnp.where(low, other, even)], axis=even.ndim - 3
    )
    return whole.reshape(-1, even.shape[-1])


def gather_whole(own):
    return lax.all_gather(own, "ctx", axis=0, tiled=True)


def plainly(multiply):
    def product(rows, weight, core, other):
        result = multiply(pick(rows, core, 1).reshape(-1, rows.shape[-1]), weight)
        return (result if other is None else result + other.astype(f32)).astype(bf16)

    return product


def scatter_rows(rows, weight, product, beside=None, ahead=None, then=None):
    ranks = lax.axis_size("ctx")
    own_rows = rows.shape[0] // ranks
    core = bit_of("ctx", 0)
    rows = rows.reshape(ranks // 2, 2, own_rows, rows.shape[1])

    other = swap(product(rows, weight, 1 - core, None), "ctx", 1)
    total = product(rows, weight, core, other)
    orders = row_orders()
    count = len(orders[0])
    halves = total.reshape((2,) * count + (2, own_rows // 2, total.shape[-1]))
    parts = [lax.index_in_dim(halves, half, count, keepdims=False) for half in range(2)]
    for step in range(count)[::-1]:
        near, far = [], []
        for part, order in zip(parts, orders):
            place = sum(bit > order[step] for bit in order[:step])
            own = bit_of("ctx", order[step])
            near.append(pick(part, own, place))
            far.append(pick(part, 1 - own, place).astype(bf16))
        others = [swap(part, "ctx", 1 << order[step]) for part, order in zip(far, orders)]
        if step == 0:
            others, beside = lax.optimization_barrier((others, beside))
        else:
            others, ahead = lax.optimization_barrier((others, ahead))
            beside = then(ahead) if then else beside
        parts = [part.astype(f32) + other.astype(f32) for part, other in zip(near, others)]
    sums = jnp.concatenate(parts)
    return sums, total, beside, ahead


def exchange_held(pieces, beside=None):
    pieces = lax.optimization_barrier(pieces)
    held = pieces[:1] + [
        swap(piece, "ctx", offset) for offset, piece in enumerate(pieces) if offset
    ]
    return lax.optimization_barrier((held, beside))


def in_order(held, axis):
    held, me = jnp.stack(held), lax.axis_index("ctx")
    return jnp.stack([pick(held, me ^ rank, 0) for rank in range(held.shape[0])], axis=axis)


def exchange(pieces, beside=None):
    me = lax.axis_index("ctx")
    pieces = [pick(pieces, me ^ offset, 0) for offset in range(pieces.shape[0])]
    shape = pieces[0].shape
    held, beside = exchange_held(pieces, beside)
    held = [piece.reshape(-1, shape[-1]) for piece in held]
    placed = place_pieces(held, me, 1, held[0].shape[0]).reshape((len(held),) + shape)
    return placed if beside is None else (placed, beside)


def body(
    tokens,
    cotangent,
    block_ids,
    attn_weight,
    gate_up,
    down_weight,
    norm_gains,
    attn_first,
    attn_second,
    gate_first,
    gate_second,
    down_first,
    down_second,
    gain_first,
    gain_second,
):
    every = ("dp", "ctx")
    width = attn_weight.shape[1] // 4
    planes = lax.axis_size("dp")
    ranks = lax.axis_size("ctx")
    own_rows = attn_weight.shape[0]
    units = down_weight.shape[0]
    rows = tokens.shape[1]
    half = rows // 2
    seq_len = rows * ranks
    local_heads = HEADS // ranks
    local_width = local_heads * HEAD
    aligned = local_heads == planes
    rank = lax.axis_index("ctx")
    top = bit_count("dp") - 1
    sharers = planes // 2
    side = bit_of("dp", top)
    hidden = sharers * units

    positions = (
        block_ids[:, None] * half + jnp.arange(half, dtype=jnp.int32)[None, :]
    ).reshape(-1)
    cosine, sine = angle_tables(positions)
    tables = (
        cosine,
        sine,
        jnp.broadcast_to(positions[:, None], (seq_len, pair_width)),
        positions[None, :],
    )

    gain_rows = 16
    grad_out_theirs = swap(cotangent[0], "dp", 1 << top)

    attn_low = attn_weight.astype(bf16)
    qkv_pieces = (
        attn_low[:, : 3 * width]
        .reshape(own_rows, 3, local_heads, ranks, HEAD)
        .transpose(3, 0, 1, 2, 4)
        .reshape(ranks, own_rows, 3 * local_width)
    )
    def cross_planes(values):
        for bit in range(top - 1):
            values = paired(values, "dp", bit)
        return values, swap(values, "dp", 1 << (top - 1))

    def join_planes(pair):
        values, other = pair
        low = bit_of("dp", top - 1) == 0
        joined = jnp.stack([jnp.where(low, values, other), jnp.where(low, other, values)])
        return joined.reshape((sharers,) + values.shape[top - 1 :])

    gains_low = norm_gains.astype(bf16)
    inputs_even = jnp.split(tokens[0], 2)
    steps = len(row_orders()[0])
    plane = lax.axis_index("dp")
    gains_low = [gains_low] + [swap(gains_low, "dp", offset) for offset in range(1, planes)]
    inputs_even, gains_low = gather_step(inputs_even, 0, gains_low)
    for step in range(1, steps - 1):
        inputs_even = gather_step(inputs_even, step)[0]
    gains_low = jnp.stack(gains_low)
    gains_own = jnp.stack([pick(gains_low, plane ^ at, 0) for at in range(planes)])
    gains_own = gains_own.reshape(planes, 2 * own_rows)
    qkv_held = exchange_held([pick(qkv_pieces, rank ^ offset, 0) for offset in range(ranks)])[0]
    inputs_even, qkv_held = gather_step(inputs_even, steps - 1, qkv_held)
    inputs_even = jnp.stack(inputs_even, axis=steps)
    qkv_own = place_pieces(qkv_held, rank, 1, own_rows).reshape(
        ranks * own_rows, 3 * local_width
    )
    up_from = gate_up.shape[1] // 2
    gate_low = gate_up.astype(bf16)

    gain_piece = jnp.pad(
        gains_own, ((0, gain_rows - planes), (0, 2 * hidden - 2 * own_rows))
    )

    def rank_columns(at):
        return jnp.concatenate(
            [
                jnp.concatenate(
                    [
                        lax.dynamic_slice_in_dim(
                            gate_low, kind * up_from + (plane * ranks + at) * units, units, 1
                        )
                        for kind in range(2)
                        for plane in range(group * sharers, (group + 1) * sharers)
                    ],
                    axis=1,
                )
                for group in range(2)
            ]
            + [gain_piece]
        )

    gate_pieces = [rank_columns(rank ^ offset) for offset in range(ranks)]
    out_low = attn_low[:, 3 * width :]
    if aligned:
        out_proj = lax.all_gather(out_low, "dp", axis=0, tiled=True)
    else:
        out_all = lax.all_gather(out_low, every, axis=0, tiled=True)
        out_proj = pick(out_all.reshape(local_heads, ranks, HEAD, width), rank, 1)
        out_proj = out_proj.reshape(local_width, width)
    qkv_own, out_proj, gate_pieces, inputs_even = lax.optimization_barrier(
        (qkv_own, out_proj, gate_pieces, inputs_even)
    )
    qkv = lax.all_gather(qkv_own, "dp", axis=0, tiled=True)
    gate_held, grad_out_theirs = exchange_held(gate_pieces, grad_out_theirs)
    gate_own = place_pieces(gate_held, rank, 2, own_rows).reshape(
        2, ranks * own_rows, 2 * hidden
    )
    gains_low = in_order(
        [held[2 * own_rows : 2 * own_rows + planes, : 2 * own_rows] for held in gate_held], 0
    )
    gains_low = gains_low.reshape(ranks, planes, 2, own_rows).transpose(2, 1, 0, 3)
    gains_low = gains_low.reshape(2, width).astype(f32)
    gain_one, gain_two = gains_low[0], gains_low[1]
    inputs_low = gather_odd(inputs_even)
    hidden_one, scale_one = normed_rows(inputs_low, gain_one)
    qkv, hidden_one, gate_own, gain_two, grad_out_own, grad_out_theirs, down = (
        lax.optimization_barrier(
            (
                qkv,
                hidden_one,
                gate_own,
                gain_two,
                cotangent[0],
                grad_out_theirs,
                down_weight.astype(bf16),
            )
        )
    )

    gate_mine = cross_planes(pick(gate_own, side, 0))
    gate_halves = jnp.split(pick(gate_own, 1 - side, 0), 2)
    gate_halves[0] = swap(gate_halves[0], "dp", 1 << top)
    grad_out_near = gather_whole(grad_out_own)
    projected = dot(hidden_one, qkv)
    queries, keys, values, mixed_low, totals = attention_forward(projected, tables)
    mixed_low, gate_mine, gate_halves, down_halves, grad_out_near, grad_out_theirs = (
        lax.optimization_barrier(
            (
                mixed_low,
                gate_mine,
                gate_halves,
                jnp.split(down, 2),
                grad_out_near,
                grad_out_theirs,
            )
        )
    )
    grad_out_far = gather_whole(grad_out_theirs)
    gate_halves[0] = cross_planes(gate_halves[0])
    gate_halves[1] = swap(gate_halves[1], "dp", 1 << top)

    inputs = tokens[0].astype(f32)
    mixed_out, _, (gate_halves, down_halves, grad_out_far), _ = scatter_rows(
        mixed_low, out_proj, plainly(dot), (gate_halves, down_halves, grad_out_far)
    )
    middle = inputs + mixed_out
    inv_two = rms_scale(middle)
    normed_two = middle * inv_two
    hidden_two_own = (normed_two * gain_two).astype(bf16)
    gate_halves[1] = cross_planes(gate_halves[1])
    down_halves[0] = cross_planes(down_halves[0])
    hidden_two_near, hidden_two_theirs, gate_halves, down_halves = lax.optimization_barrier(
        (
            gather_whole(hidden_two_own),
            swap(hidden_two_own, "dp", 1 << top),
            gate_halves,
            down_halves,
        ),
    )
    down_halves[1] = cross_planes(down_halves[1])
    gate_mine = join_planes(gate_mine)
    gate_theirs = jnp.concatenate([join_planes(pair) for pair in gate_halves], axis=1)
    down = jnp.concatenate([join_planes(pair) for pair in down_halves], axis=1)
    down = down.reshape(hidden, width)
    hidden_two_far = gather_whole(hidden_two_theirs)
    grad_outs = [grad_out_near, grad_out_far]
    gate = jnp.concatenate(
        [
            jnp.where(side == 0, gate_mine, gate_theirs),
            jnp.where(side == 0, gate_theirs, gate_mine),
        ]
    ).reshape(width, 2 * hidden)

    activation_near, grad_both_near = swiglu(
        dot(hidden_two_near, gate), contract_last(grad_outs[0], down)
    )
    grad_two, _, _, far_inputs = scatter_rows(
        grad_both_near, gate, plainly(contract_last), ahead=(hidden_two_far, grad_outs[1])
    )
    hidden_two_far, grad_outs[1] = far_inputs
    gate_both, grad_two = lax.optimization_barrier((dot(hidden_two_far, gate), grad_two))
    activation_far, grad_both_far = swiglu(gate_both, contract_last(grad_outs[1], down))
    activations = [activation_near, activation_far]
    hidden_twos = [hidden_two_near, hidden_two_far]
    grad_boths = [grad_both_near, grad_both_far]

    def gate_terms(group):
        rows_in_group = width // 2
        terms = sum(
            contract_first(
                lax.dynamic_slice_in_dim(hidden_two, group * rows_in_group, rows_in_group, 1),
                grad_both,
            )
            for hidden_two, grad_both in zip(hidden_twos, grad_boths)
        )
        return terms.astype(bf16).reshape(sharers, ranks * own_rows, 2 * hidden)

    def sum_planes(values):
        for bit in range(top)[::-1]:
            values = halved(values.astype(bf16), "dp", bit)
        return values[0]

    grad_two_far, started, _, _ = scatter_rows(grad_both_far, gate, plainly(contract_last))
    hidden_twos, grad_boths, activations, started = lax.optimization_barrier(
        (hidden_twos, grad_boths, activations, started)
    )
    down_term = sum(contract_first(a, g) for a, g in zip(activations, grad_outs)).astype(bf16)
    term_theirs = sum_planes(gate_terms(1 - side)).astype(bf16)
    grad_two += swap(grad_two_far.astype(bf16), "dp", 1 << top).astype(f32)
    term_mine = gate_terms(side)
    grad_two, term_mine, term_theirs, down_term, activations = lax.optimization_barrier(
        (grad_two, term_mine, term_theirs, down_term, activations)
    )
    theirs_parts = thirds(term_theirs, 0)
    down_parts = thirds(down_term.reshape(sharers, units, width), 1)
    def cross(parts, at):
        theirs, downs = list(parts[0]), list(parts[1])
        theirs[at] = swap(theirs[at], "dp", 1 << top)
        downs[at] = sum_planes(downs[at])
        return theirs, downs

    reduced_two = grad_two * gain_two
    grad_gain_two = jnp.sum(grad_two * normed_two, axis=0)
    grad_after = cotangent[0].astype(f32) + inv_two * (
        reduced_two - normed_two * jnp.mean(reduced_two * normed_two, axis=-1, keepdims=True)
    )
    after_low = gather_whole(grad_after.astype(bf16))
    output_far, _, parts, _ = scatter_rows(
        activations[1],
        down,
        plainly(dot),
        ahead=cross((theirs_parts, down_parts), 0),
        then=lambda parts: cross(parts, 1),
    )
    grad_mixed = contract_last(after_low, out_proj).astype(bf16)
    grad_mixed, mixed_low, after_low, term_mine, parts, output_far = lax.optimization_barrier(
        (grad_mixed, mixed_low, after_low, term_mine, parts, output_far)
    )
    parts = cross(parts, 2)
    term_mine = sum_planes(term_mine).astype(bf16)
    grad_parts = attention_backward(queries, keys, values, grad_mixed, totals, tables)
    grad_parts, term_mine, parts = lax.optimization_barrier((grad_parts, term_mine, parts))
    term_theirs = jnp.concatenate(parts[0])
    down_grad = jnp.concatenate(parts[1])
    grad_proj = jnp.concatenate(grad_parts, axis=1)
    qkv_term = contract_first(hidden_one, grad_proj).astype(bf16)
    out_term = contract_first(mixed_low, after_low).astype(bf16)
    if aligned:
        out_term = out_term.reshape(width, local_width)
        qkv_term = jnp.concatenate([qkv_term, out_term], axis=1)
    else:
        spread = jnp.zeros((local_heads, ranks, HEAD, width), bf16)
        spread = lax.dynamic_update_index_in_dim(
            spread, out_term.reshape(local_heads, 1, HEAD, width), rank, 1
        )
        out_grad = lax.psum_scatter(
            spread.reshape(HEADS * HEAD, width), every, scatter_dimension=0, tiled=True
        )
    grad_proj, qkv_term, inputs_low, activation_near = lax.optimization_barrier(
        (grad_proj, qkv_term, inputs_low, activations[0])
    )
    qkv_term = lax.psum_scatter(qkv_term, "dp", scatter_dimension=0, tiled=True)
    if aligned:
        out_grad = qkv_term[:, 3 * local_width :].reshape(own_rows, width)
        qkv_term = qkv_term[:, : 3 * local_width]
    out_grad = out_grad.astype(f32)
    gain_one_parts = []

    def gained(*operands):
        product, gain = core_product(*operands, True, (inputs_low, scale_one))
        gain_one_parts.append(gain.reshape(width))
        return product

    grad_one = scatter_rows(grad_proj, qkv, gained)[0]
    grad_gain_one = sum(gain_one_parts)
    inv_one = rms_scale(inputs)
    normed_one = inputs * inv_one
    reduced_one = grad_one * gain_one
    grad_input = grad_after + inv_one * (
        reduced_one - normed_one * jnp.mean(reduced_one * normed_one, axis=-1, keepdims=True)
    )

    output_near = scatter_rows(
        activation_near, down, lambda *operands: core_product(*operands, False)[0]
    )[0]
    term_cols = jnp.stack(
        [
            jnp.where(side == 0, term_mine, term_theirs),
            jnp.where(side == 0, term_theirs, term_mine),
        ]
    )
    term_cols = term_cols.reshape(2, ranks, own_rows, 2 * hidden).transpose(1, 0, 2, 3)
    gate_pieces = exchange(term_cols)
    gain_grad = jnp.stack([grad_gain_one, grad_gain_two]).reshape(2, planes, ranks, -1)
    gain_grad = gain_grad.transpose(2, 1, 0, 3)
    for bit in range(bit_count("ctx"))[::-1]:
        gain_grad = halved(gain_grad, "ctx", bit)
    gate_stepped = gate_step(
        gate_pieces, gate_up, gate_first, gate_second, 3.0 / math.sqrt(D), sharers, units
    )
    down_stepped = plain_step(
        down_grad, down_weight, down_first, down_second, 3.0 / math.sqrt(FF)
    )
    held_back = (gate_stepped, down_stepped, output_near, output_far, grad_input, gain_grad)
    qkv_term, out_grad, held_back = lax.optimization_barrier((qkv_term, out_grad, held_back))
    gate_stepped, down_stepped, output_near, output_far, grad_input, gain_grad = held_back
    gate_grad, gate_new, gate_moment, gate_square = gate_stepped
    down_grad, down_new, down_moment, down_square = down_stepped
    output_far = output_far.astype(bf16)
    gain_parts = [pick(gain_grad[0], plane ^ offset, 0) for offset in range(planes)]
    qkv_pieces, output_far = exchange(
        qkv_term.reshape(ranks, own_rows, 3 * local_width), swap(output_far, "dp", 1 << top)
    )
    gain_parts, output_far = lax.optimization_barrier((gain_parts, output_far))
    outputs = middle + output_near + output_far.astype(f32)
    gain_grad = sum(
        gain_parts[:1]
        + [swap(part, "dp", offset) for offset, part in enumerate(gain_parts) if offset]
    )
    gain_grad = gain_grad.reshape(2, -1)
    attn_grad, attn_new, attn_moment, attn_square = attn_step(
        qkv_pieces, out_grad, attn_weight, attn_first, attn_second, 3.0 / math.sqrt(D)
    )
    gain_new, gain_moment, gain_square = adam_step(
        norm_gains, gain_grad, gain_first, gain_second, gain_rate, 0.0
    )
    return (
        outputs.astype(bf16)[None],
        grad_input.astype(bf16)[None],
        attn_grad,
        gate_grad,
        down_grad,
        gain_grad,
        attn_new,
        gate_new,
        down_new,
        gain_new,
        attn_moment,
        gate_moment,
        down_moment,
        gain_moment,
        attn_square,
        gate_square,
        down_square,
        gain_square,
    )


def solution(mesh):
    acts = P("dp", "ctx", None)
    weight = P(("dp", "ctx"), None)
    gains = P(None, ("dp", "ctx"))
    four = (weight, weight, weight, gains)
    return jax.shard_map(
        body,
        mesh=mesh,
        in_specs=(acts, acts, P()) + four + (weight,) * 6 + (gains,) * 2,
        out_specs=(acts, acts) + four * 4,
        check_vma=False,
    )
```

```python
import math

import jax
import jax.numpy as jnp
from jax import lax
from jax.experimental import pallas as pl
from jax.experimental.pallas import tpu as pltpu
from jax.sharding import PartitionSpec as P

D = 2048
HEADS = 32
HEAD = 64
FF = 8192
STEP = 5

norm_eps = 1e-05
rope_base = 130000.0
beta_one = 0.9
beta_two = 0.95
adam_eps = 1e-08
decay_rate = 0.1
gain_rate = 0.4
masked = -1e30
score_scale = HEAD ** (-0.5)
pair_width = 2 * HEAD
query_block = 256

bf16 = jnp.bfloat16
f32 = jnp.float32

light = pl.CostEstimate(flops=0, bytes_accessed=0, transcendentals=0)


def rms_scale(values):
    return lax.rsqrt(jnp.mean(values * values, axis=-1, keepdims=True) + norm_eps)


def angle_tables(positions):
    index = jnp.arange(HEAD // 2, dtype=f32)
    freqs = jnp.power(f32(rope_base), -2.0 * index / HEAD)
    phase = positions.astype(f32)[:, None] * freqs[None, :]
    return jnp.tile(jnp.cos(phase), (1, 4)), jnp.tile(jnp.sin(phase), (1, 4))


def dot(first, second):
    return jnp.dot(first, second, preferred_element_type=f32)


def contract_last(first, second):
    return lax.dot_general(first, second, (((1,), (1,)), ((), ())), preferred_element_type=f32)


def contract_first(first, second):
    return lax.dot_general(first, second, (((0,), (0,)), ((), ())), preferred_element_type=f32)


def thirds(values, axis):
    size = values.shape[axis] // 16
    first = -(-size // 3)
    second = first + (size - first + 1) // 2
    return jnp.split(values, [16 * first, 16 * second], axis=axis)


def adam_step(weight, grad, first, second, rate, decay):
    first = beta_one * first + (1.0 - beta_one) * grad
    second = beta_two * second + (1.0 - beta_two) * grad * grad
    corrected_first = first / (1.0 - beta_one**STEP)
    corrected_second = second / (1.0 - beta_two**STEP)
    fresh = weight - rate * (
        corrected_first / (jnp.sqrt(corrected_second) + adam_eps) + decay * weight
    )
    return (fresh, first, second)


def swiglu(gate_both, grad_act):
    rows, columns = gate_both.shape
    hidden = columns // 2
    block = 256

    def kernel(gate_ref, grad_ref, activation_out, grad_out):
        gate_part, up_part = gate_ref[:, :hidden], gate_ref[:, hidden:]
        grad = grad_ref[...]
        sigmoid = jax.nn.sigmoid(gate_part)
        gate_act = gate_part * sigmoid
        activation_out[...] = (gate_act * up_part).astype(bf16)
        grad_out[:, :hidden] = (
            grad * up_part * sigmoid * (1.0 + gate_part * (1.0 - sigmoid))
        ).astype(bf16)
        grad_out[:, hidden:] = (grad * gate_act).astype(bf16)

    def spec(width):
        return pl.BlockSpec((block, width), lambda step: (step, 0))

    return pl.pallas_call(
        kernel,
        grid=(rows // block,),
        in_specs=[spec(columns), spec(hidden)],
        out_specs=[spec(hidden), spec(columns)],
        out_shape=[
            jax.ShapeDtypeStruct((rows, hidden), bf16),
            jax.ShapeDtypeStruct((rows, columns), bf16),
        ],
        compiler_params=pltpu.CompilerParams(vmem_limit_bytes=40 * 2**20),
        cost_estimate=light,
        name="swiglu",
    )(gate_both, grad_act)


def normed_rows(inputs, gain):
    rows, width = inputs.shape
    block = 256

    def kernel(inputs_ref, gain_ref, normed_out, scale_out):
        values = inputs_ref[...].astype(f32)
        scale = rms_scale(values)
        normed_out[...] = (values * scale * gain_ref[...]).astype(bf16)
        scale_out[...] = jnp.broadcast_to(scale, scale_out.shape)

    spec = pl.BlockSpec((block, width), lambda step: (step, 0))
    return pl.pallas_call(
        kernel,
        grid=(rows // block,),
        in_specs=[spec, pl.BlockSpec((1, width), lambda step: (0, 0))],
        out_specs=[spec, pl.BlockSpec((block, 128), lambda step: (step, 0))],
        out_shape=[
            jax.ShapeDtypeStruct((rows, width), bf16),
            jax.ShapeDtypeStruct((rows, 128), f32),
        ],
        compiler_params=pltpu.CompilerParams(vmem_limit_bytes=40 * 2**20),
        cost_estimate=light,
        name="normed_rows",
    )(inputs, gain.reshape(1, width))


def place_pieces(held, rank, groups, rows):
    ranks, columns = len(held), held[0].shape[1]

    def kernel(rank_ref, *refs):
        out_ref = refs[ranks]
        for group in range(groups):
            for offset in range(ranks):
                piece = refs[offset][group * rows : (group + 1) * rows]
                out_ref[group, rank_ref[0] ^ offset] = piece

    return pl.pallas_call(
        kernel,
        in_specs=[pl.BlockSpec(memory_space=pltpu.SMEM)]
        + [pl.BlockSpec(memory_space=pltpu.VMEM)] * ranks,
        out_specs=pl.BlockSpec(memory_space=pltpu.VMEM),
        out_shape=jax.ShapeDtypeStruct((groups, ranks, rows, columns), held[0].dtype),
        compiler_params=pltpu.CompilerParams(vmem_limit_bytes=40 * 2**20),
        cost_estimate=light,
        name="place_pieces",
    )(rank.reshape(1), *held)


def core_product(rows, weight, core, other, transposed, normed=None):
    groups, _, own_rows, depth = rows.shape
    width = weight.shape[0] if transposed else weight.shape[1]
    count, block = groups * own_rows, 512

    def kernel(core_ref, rows_ref, weight_ref, *refs):
        refs = list(refs)
        part = rows_ref[...].reshape(count, depth)
        contract = ((1,), (1,)) if transposed else ((1,), (0,))
        product = lax.dot_general(
            part, weight_ref[...], (contract, ((), ())), preferred_element_type=f32
        )
        if normed is not None:
            inputs_ref, scale_ref, gain_out = refs.pop(0), refs.pop(0), refs.pop()
            values = inputs_ref[...].reshape(count, block).astype(f32)
            scale = scale_ref[...].reshape(count, 128)[:, :1]
            gain_out[...] = jnp.sum(product * (values * scale), axis=0, keepdims=True)
        if other is not None:
            product += refs.pop(0)[...].astype(f32)
        refs[0][...] = product.astype(bf16)

    def of_core(columns, moving):
        return pl.BlockSpec(
            (groups, 1, own_rows, columns),
            lambda step, core_ref: (0, core_ref[0], 0, step if moving else 0),
        )

    operands = [rows, weight]
    in_specs = [
        of_core(depth, False),
        pl.BlockSpec((block, depth), lambda step, core_ref: (step, 0))
        if transposed
        else pl.BlockSpec((depth, block), lambda step, core_ref: (0, step)),
    ]
    column = pl.BlockSpec((count, block), lambda step, core_ref: (0, step))
    out_specs, out_shape = [column], [jax.ShapeDtypeStruct((count, width), bf16)]
    if normed is not None:
        operands += [values.reshape(groups, 2, own_rows, -1) for values in normed]
        in_specs += [of_core(block, True), of_core(128, False)]
        out_specs.append(pl.BlockSpec((1, block), lambda step, core_ref: (0, step)))
        out_shape.append(jax.ShapeDtypeStruct((1, width), f32))
    if other is not None:
        operands.append(other)
        in_specs.append(column)
    return pl.pallas_call(
        kernel,
        grid_spec=pltpu.PrefetchScalarGridSpec(
            num_scalar_prefetch=1,
            grid=(width // block,),
            in_specs=in_specs,
            out_specs=out_specs,
        ),
        out_shape=out_shape,
        compiler_params=pltpu.CompilerParams(vmem_limit_bytes=40 * 2**20),
        cost_estimate=light,
        name="core_product",
    )(core.reshape(1), *operands)


def write_step(refs, grad, rate):
    weight_ref, first_ref, second_ref, grad_out, new_out, moment_out, square_out = refs
    fresh, first, second = adam_step(
        weight_ref[...], grad, first_ref[...], second_ref[...], rate, decay_rate
    )
    grad_out[...] = grad
    new_out[...] = fresh
    moment_out[...] = first
    square_out[...] = second


def plain_step(grad, weight, first, second, rate):
    rows, width = weight.shape
    block = pl.BlockSpec((rows // 4, width), lambda step: (step, 0))

    def kernel(grad_ref, *refs):
        write_step(refs, grad_ref[...], rate)

    return pl.pallas_call(
        kernel,
        grid=(4,),
        in_specs=[block] * 4,
        out_specs=[block] * 4,
        out_shape=[jax.ShapeDtypeStruct(weight.shape, f32)] * 4,
        compiler_params=pltpu.CompilerParams(vmem_limit_bytes=40 * 2**20),
        cost_estimate=light,
        name="plain_step",
    )(grad, weight, first, second)


def gate_step(pieces, weight, first, second, rate, sharers, units):
    ranks, groups, rows, _ = pieces.shape
    block = pl.BlockSpec(
        (rows, sharers * ranks * units), lambda kind, group: (0, kind * groups + group)
    )

    def kernel(pieces_ref, *refs):
        parts = [pieces_ref[rank, 0].astype(f32) for rank in range(ranks)]
        grad = jnp.concatenate(
            [
                part[:, plane * units : (plane + 1) * units]
                for plane in range(sharers)
                for part in parts
            ],
            axis=1,
        )
        write_step(refs, grad, rate)

    return pl.pallas_call(
        kernel,
        grid=(2, groups),
        in_specs=[
            pl.BlockSpec(
                (ranks, 1, rows, sharers * units),
                lambda kind, group: (0, group, 0, kind),
            )
        ]
        + [block] * 3,
        out_specs=[block] * 4,
        out_shape=[jax.ShapeDtypeStruct(weight.shape, f32)] * 4,
        compiler_params=pltpu.CompilerParams(vmem_limit_bytes=40 * 2**20),
        cost_estimate=pl.CostEstimate(
            flops=2**12 * weight.size, bytes_accessed=weight.size, transcendentals=0
        ),
        name="gate_step",
    )(pieces, weight, first, second)


def attn_step(pieces, out_grad, weight, first, second, rate):
    ranks, rows, columns = pieces.shape
    local_width = columns // 3
    block = pl.BlockSpec((rows, ranks * local_width), lambda kind: (0, kind))

    def kernel(pieces_ref, out_ref, *refs):
        kind = pl.program_id(0)

        @pl.when(kind < 3)
        def _():
            parts = [pieces_ref[rank].astype(f32) for rank in range(ranks)]
            grad = jnp.concatenate(
                [
                    part[:, start : start + HEAD]
                    for start in range(0, local_width, HEAD)
                    for part in parts
                ],
                axis=1,
            )
            write_step(refs, grad, rate)

        @pl.when(kind == 3)
        def _():
            write_step(refs, out_ref[...], rate)

    return pl.pallas_call(
        kernel,
        grid=(4,),
        in_specs=[
            pl.BlockSpec((ranks, rows, local_width), lambda kind: (0, 0, jnp.minimum(kind, 2))),
            pl.BlockSpec((rows, ranks * local_width), lambda kind: (0, 0)),
        ]
        + [block] * 3,
        out_specs=[block] * 4,
        out_shape=[jax.ShapeDtypeStruct(weight.shape, f32)] * 4,
        compiler_params=pltpu.CompilerParams(vmem_limit_bytes=40 * 2**20),
        cost_estimate=light,
        name="attn_step",
    )(pieces, out_grad, weight, first, second)


def first_half(shape):
    return lax.broadcasted_iota(jnp.int32, shape, 1) % HEAD < HEAD // 2


def of_head(values, head, axis=1):
    return jnp.where(
        lax.broadcasted_iota(jnp.int32, values.shape, axis) // HEAD == head,
        values,
        jnp.zeros_like(values),
    )


def rotate(values, cosine, sine):
    ahead = pltpu.roll(values, pair_width - HEAD // 2, 1)
    behind = pltpu.roll(values, HEAD // 2, 1)
    return values * cosine + jnp.where(first_half(values.shape), -ahead, behind) * sine


def unrotate(values, cosine, sine):
    sined = values * sine
    ahead = pltpu.roll(sined, pair_width - HEAD // 2, 1)
    behind = pltpu.roll(sined, HEAD // 2, 1)
    return values * cosine + jnp.where(first_half(values.shape), ahead, -behind)


def forward_kernel(
    query_ref,
    key_ref,
    value_ref,
    cos_rows,
    sin_rows,
    cos_ref,
    sin_ref,
    key_pos,
    query_pos,
    query_out,
    key_out,
    value_out,
    mixed_out,
    total_out,
):
    @pl.when(pl.program_id(1) == 0)
    def _():
        key_out[...] = rotate(key_ref[...], cos_ref[...], sin_ref[...]).astype(bf16)
        value_out[...] = value_ref[...].astype(bf16)

    queries = rotate(query_ref[...], cos_rows[...], sin_rows[...]).astype(bf16)
    query_out[...] = queries
    keys, values = key_out[...], value_out[...]
    allowed = key_pos[:, :1] <= query_pos[...]
    mixed = jnp.zeros((pair_width, queries.shape[0]), f32)
    for head in range(2):
        scores = contract_last(keys, of_head(queries, head) * bf16(score_scale))
        scores = jnp.where(allowed, scores, masked)
        peak = jnp.max(scores, axis=0, keepdims=True)
        weights = jnp.exp(scores - peak)
        total = jnp.sum(weights, axis=0, keepdims=True)
        probs = (weights * (1.0 / total)).astype(bf16)
        mixed += of_head(contract_first(values, probs), head, 0)
        total_out[head] = peak + jnp.log(total)
    mixed_out[...] = mixed.T.astype(bf16)


def backward_kernel(
    query_ref,
    key_ref,
    value_ref,
    grad_ref,
    total_ref,
    cos_rows,
    sin_rows,
    cos_ref,
    sin_ref,
    key_pos,
    query_pos,
    query_out,
    key_out,
    value_out,
    key_sum,
    value_sum,
):
    step = pl.program_id(1)

    @pl.when(step == 0)
    def _():
        key_sum[...] = jnp.zeros_like(key_sum)
        value_sum[...] = jnp.zeros_like(value_sum)

    keys, values = key_ref[...], value_ref[...]
    allowed = key_pos[:, :1] <= query_pos[...]
    grad_query = jnp.zeros((pair_width, query_ref.shape[0]), f32)
    for head in range(2):
        queries = of_head(query_ref[...], head) * bf16(score_scale)
        grads = of_head(grad_ref[...], head)
        scores = jnp.where(allowed, contract_last(keys, queries), masked)
        probs = jnp.exp(scores - total_ref[head])
        grad_probs = contract_last(values, grads)
        delta = jnp.sum(probs * grad_probs, axis=0, keepdims=True)
        grad_scores = (probs * (grad_probs - delta)).astype(bf16)
        value_sum[...] += dot(probs.astype(bf16), grads)
        key_sum[...] += dot(grad_scores, queries)
        grad_query += of_head(contract_first(keys, grad_scores), head, 0)
    query_out[...] = unrotate(
        (grad_query * score_scale).T, cos_rows[...], sin_rows[...]
    ).astype(bf16)

    @pl.when(step == pl.num_programs(1) - 1)
    def _():
        key_out[...] = unrotate(key_sum[...], cos_ref[...], sin_ref[...]).astype(bf16)
        value_out[...] = value_sum[...].astype(bf16)


def attention_specs(seq_len, pairs):
    rows = pl.BlockSpec((query_block, pair_width), lambda pair, step: (step, pair))
    whole = [
        pl.BlockSpec((seq_len, pair_width), lambda pair, step, at=at: (0, at * pairs + pair))
        for at in range(3)
    ]
    tables = [pl.BlockSpec((query_block, pair_width), lambda pair, step: (step, 0))] * 2 + [
        pl.BlockSpec((seq_len, pair_width), lambda pair, step: (0, 0))
    ] * 3
    places = pl.BlockSpec((1, query_block), lambda pair, step: (0, step))
    totals = pl.BlockSpec((2, 1, query_block), lambda pair, step: (pair, 0, step))
    return rows, whole, tables + [places], totals


def attention_forward(projected, tables):
    seq_len = projected.shape[0]
    pairs = projected.shape[1] // 3 // pair_width
    rows, whole, table_specs, totals = attention_specs(seq_len, pairs)
    low = jax.ShapeDtypeStruct((seq_len, pairs * pair_width), bf16)
    cosine, sine, key_pos, query_pos = tables
    return pl.pallas_call(
        forward_kernel,
        grid=(pairs, seq_len // query_block),
        in_specs=[rows, whole[1], whole[2]] + table_specs,
        out_specs=[rows, whole[0], whole[0], rows, totals],
        out_shape=[low] * 4 + [jax.ShapeDtypeStruct((2 * pairs, 1, seq_len), f32)],
        compiler_params=pltpu.CompilerParams(vmem_limit_bytes=40 * 2**20),
        cost_estimate=light,
        name="attention_forward",
    )(projected, projected, projected, cosine, sine, cosine, sine, key_pos, query_pos)


def attention_backward(queries, keys, values, grads, totals, tables):
    seq_len = queries.shape[0]
    pairs = queries.shape[1] // pair_width
    rows, whole, table_specs, total_spec = attention_specs(seq_len, pairs)
    low = jax.ShapeDtypeStruct((seq_len, pairs * pair_width), bf16)
    cosine, sine, key_pos, query_pos = tables
    return pl.pallas_call(
        backward_kernel,
        grid=(pairs, seq_len // query_block),
        in_specs=[rows, whole[0], whole[0], rows, total_spec] + table_specs,
        out_specs=[rows, whole[0], whole[0]],
        out_shape=[low] * 3,
        scratch_shapes=[pltpu.VMEM((seq_len, pair_width), f32)] * 2,
        compiler_params=pltpu.CompilerParams(vmem_limit_bytes=40 * 2**20),
        cost_estimate=light,
        name="attention_backward",
    )(queries, keys, values, grads, totals, cosine, sine, cosine, sine, key_pos, query_pos)


def swap(values, axis, bits):
    return lax.ppermute(values, axis, [(i, i ^ bits) for i in range(lax.axis_size(axis))])


def bit_of(axis, bit):
    return (lax.axis_index(axis) >> bit) & 1


def pick(values, index, axis):
    return lax.dynamic_index_in_dim(values, index, axis, keepdims=False)


def bit_count(axis):
    return lax.axis_size(axis).bit_length() - 1


def paired(values, axis, bit):
    other = swap(values, axis, 1 << bit)
    mine = bit_of(axis, bit) == 0
    return jnp.stack([jnp.where(mine, values, other), jnp.where(mine, other, values)])


def halved(values, axis, bit):
    values = values.reshape((2, values.shape[0] // 2) + values.shape[1:])
    own = bit_of(axis, bit)
    other = swap(pick(values, 1 - own, 0), axis, 1 << bit)
    return pick(values, own, 0).astype(f32) + other.astype(f32)


def after(values, *others):
    return lax.optimization_barrier((values, others))[0]


def row_orders():
    bits = list(range(1, bit_count("ctx")))
    return bits, bits[::-1]


def gather_step(parts, step, beside=None):
    orders = row_orders()
    others = [swap(part, "ctx", 1 << order[step]) for part, order in zip(parts, orders)]
    others, beside = lax.optimization_barrier((others, beside))
    merged = []
    for part, other, order in zip(parts, others, orders):
        low = bit_of("ctx", order[step]) == 0
        place = sum(bit > order[step] for bit in order[:step])
        merged.append(
            jnp.stack([jnp.where(low, part, other), jnp.where(low, other, part)], axis=place)
        )
    return merged, beside


def gather_odd(even):
    other = swap(even, "ctx", 1)
    low = bit_of("ctx", 0) == 0
    whole = jnp.stack(
        [jnp.where(low, even, other), jnp.where(low, other, even)], axis=even.ndim - 3
    )
    return whole.reshape(-1, even.shape[-1])


def gather_whole(own):
    return lax.all_gather(own, "ctx", axis=0, tiled=True)


def plainly(multiply):
    def product(rows, weight, core, other):
        result = multiply(pick(rows, core, 1).reshape(-1, rows.shape[-1]), weight)
        return (result if other is None else result + other.astype(f32)).astype(bf16)

    return product


def scatter_rows(rows, weight, product, beside=None, ahead=None, then=None):
    ranks = lax.axis_size("ctx")
    own_rows = rows.shape[0] // ranks
    core = bit_of("ctx", 0)
    rows = rows.reshape(ranks // 2, 2, own_rows, rows.shape[1])

    other = swap(product(rows, weight, 1 - core, None), "ctx", 1)
    total = product(rows, weight, core, other)
    orders = row_orders()
    count = len(orders[0])
    halves = total.reshape((2,) * count + (2, own_rows // 2, total.shape[-1]))
    parts = [lax.index_in_dim(halves, half, count, keepdims=False) for half in range(2)]
    for step in range(count)[::-1]:
        near, far = [], []
        for part, order in zip(parts, orders):
            place = sum(bit > order[step] for bit in order[:step])
            own = bit_of("ctx", order[step])
            near.append(pick(part, own, place))
            far.append(pick(part, 1 - own, place).astype(bf16))
        others = [swap(part, "ctx", 1 << order[step]) for part, order in zip(far, orders)]
        if step == 0:
            others, beside = lax.optimization_barrier((others, beside))
        else:
            others, ahead = lax.optimization_barrier((others, ahead))
            beside = then(ahead) if then else beside
        parts = [part.astype(f32) + other.astype(f32) for part, other in zip(near, others)]
    sums = jnp.concatenate(parts)
    return sums, total, beside, ahead


def exchange_held(pieces, beside=None):
    pieces = lax.optimization_barrier(pieces)
    held = pieces[:1] + [
        swap(piece, "ctx", offset) for offset, piece in enumerate(pieces) if offset
    ]
    return lax.optimization_barrier((held, beside))


def in_order(held, axis):
    held, me = jnp.stack(held), lax.axis_index("ctx")
    return jnp.stack([pick(held, me ^ rank, 0) for rank in range(held.shape[0])], axis=axis)


def exchange(pieces, beside=None):
    me = lax.axis_index("ctx")
    pieces = [pick(pieces, me ^ offset, 0) for offset in range(pieces.shape[0])]
    shape = pieces[0].shape
    held, beside = exchange_held(pieces, beside)
    held = [piece.reshape(-1, shape[-1]) for piece in held]
    placed = place_pieces(held, me, 1, held[0].shape[0]).reshape((len(held),) + shape)
    return placed if beside is None else (placed, beside)


def body(
    tokens,
    cotangent,
    block_ids,
    attn_weight,
    gate_up,
    down_weight,
    norm_gains,
    attn_first,
    attn_second,
    gate_first,
    gate_second,
    down_first,
    down_second,
    gain_first,
    gain_second,
):
    every = ("dp", "ctx")
    width = attn_weight.shape[1] // 4
    planes = lax.axis_size("dp")
    ranks = lax.axis_size("ctx")
    own_rows = attn_weight.shape[0]
    units = down_weight.shape[0]
    rows = tokens.shape[1]
    half = rows // 2
    seq_len = rows * ranks
    local_heads = HEADS // ranks
    local_width = local_heads * HEAD
    aligned = local_heads == planes
    rank = lax.axis_index("ctx")
    top = bit_count("dp") - 1
    sharers = planes // 2
    side = bit_of("dp", top)
    hidden = sharers * units

    positions = (
        block_ids[:, None] * half + jnp.arange(half, dtype=jnp.int32)[None, :]
    ).reshape(-1)
    cosine, sine = angle_tables(positions)
    tables = (
        cosine,
        sine,
        jnp.broadcast_to(positions[:, None], (seq_len, pair_width)),
        positions[None, :],
    )

    gain_rows = 16
    grad_out_theirs = swap(cotangent[0], "dp", 1 << top)

    attn_low = attn_weight.astype(bf16)
    qkv_pieces = (
        attn_low[:, : 3 * width]
        .reshape(own_rows, 3, local_heads, ranks, HEAD)
        .transpose(3, 0, 1, 2, 4)
        .reshape(ranks, own_rows, 3 * local_width)
    )
    def cross_planes(values):
        for bit in range(top - 1):
            values = paired(values, "dp", bit)
        return values, swap(values, "dp", 1 << (top - 1))

    def join_planes(pair):
        values, other = pair
        low = bit_of("dp", top - 1) == 0
        joined = jnp.stack([jnp.where(low, values, other), jnp.where(low, other, values)])
        return joined.reshape((sharers,) + values.shape[top - 1 :])

    gains_low = norm_gains.astype(bf16)
    inputs_even = jnp.split(tokens[0], 2)
    steps = len(row_orders()[0])
    plane = lax.axis_index("dp")
    gains_low = [gains_low] + [swap(gains_low, "dp", offset) for offset in range(1, planes)]
    inputs_even, gains_low = gather_step(inputs_even, 0, gains_low)
    for step in range(1, steps - 1):
        inputs_even = gather_step(inputs_even, step)[0]
    gains_low = jnp.stack(gains_low)
    gains_own = jnp.stack([pick(gains_low, plane ^ at, 0) for at in range(planes)])
    gains_own = gains_own.reshape(planes, 2 * own_rows)
    qkv_held = exchange_held([pick(qkv_pieces, rank ^ offset, 0) for offset in range(ranks)])[0]
    inputs_even, qkv_held = gather_step(inputs_even, steps - 1, qkv_held)
    inputs_even = jnp.stack(inputs_even, axis=steps)
    qkv_own = place_pieces(qkv_held, rank, 1, own_rows).reshape(
        ranks * own_rows, 3 * local_width
    )
    up_from = gate_up.shape[1] // 2
    gate_low = gate_up.astype(bf16)

    gain_piece = jnp.pad(
        gains_own, ((0, gain_rows - planes), (0, 2 * hidden - 2 * own_rows))
    )

    def rank_columns(at):
        return jnp.concatenate(
            [
                jnp.concatenate(
                    [
                        lax.dynamic_slice_in_dim(
                            gate_low, kind * up_from + (plane * ranks + at) * units, units, 1
                        )
                        for kind in range(2)
                        for plane in range(group * sharers, (group + 1) * sharers)
                    ],
                    axis=1,
                )
                for group in range(2)
            ]
            + [gain_piece]
        )

    gate_pieces = [rank_columns(rank ^ offset) for offset in range(ranks)]
    out_low = attn_low[:, 3 * width :]
    if aligned:
        out_proj = lax.all_gather(out_low, "dp", axis=0, tiled=True)
    else:
        out_all = lax.all_gather(out_low, every, axis=0, tiled=True)
        out_proj = pick(out_all.reshape(local_heads, ranks, HEAD, width), rank, 1)
        out_proj = out_proj.reshape(local_width, width)
    qkv_own, out_proj, gate_pieces, inputs_even = lax.optimization_barrier(
        (qkv_own, out_proj, gate_pieces, inputs_even)
    )
    qkv = lax.all_gather(qkv_own, "dp", axis=0, tiled=True)
    gate_held, grad_out_theirs = exchange_held(gate_pieces, grad_out_theirs)
    gate_own = place_pieces(gate_held, rank, 2, own_rows).reshape(
        2, ranks * own_rows, 2 * hidden
    )
    gains_low = in_order(
        [held[2 * own_rows : 2 * own_rows + planes, : 2 * own_rows] for held in gate_held], 0
    )
    gains_low = gains_low.reshape(ranks, planes, 2, own_rows).transpose(2, 1, 0, 3)
    gains_low = gains_low.reshape(2, width).astype(f32)
    gain_one, gain_two = gains_low[0], gains_low[1]
    inputs_low = gather_odd(inputs_even)
    hidden_one, scale_one = normed_rows(inputs_low, gain_one)
    gate_mine = pick(gate_own, side, 0)
    gate_halves = jnp.split(pick(gate_own, 1 - side, 0), 2)
    hidden_one, tables, scale_one = lax.optimization_barrier((hidden_one, tables, scale_one))
    qkv, hidden_one, gate_mine, gate_halves, gain_two, grad_out_own, grad_out_theirs, down = (
        lax.optimization_barrier(
            (
                qkv,
                hidden_one,
                gate_mine,
                gate_halves,
                gain_two,
                cotangent[0],
                grad_out_theirs,
                down_weight.astype(bf16),
            )
        )
    )
    gate_mine = cross_planes(gate_mine)
    gate_halves[0] = swap(gate_halves[0], "dp", 1 << top)
    grad_out_near = gather_whole(grad_out_own)
    projected = dot(hidden_one, qkv)
    queries, keys, values, mixed_low, totals = attention_forward(projected, tables)
    mixed_low, gate_mine, gate_halves, down_halves, grad_out_near, grad_out_theirs = (
        lax.optimization_barrier(
            (
                mixed_low,
                gate_mine,
                gate_halves,
                jnp.split(down, 2),
                grad_out_near,
                grad_out_theirs,
            )
        )
    )
    grad_out_far = gather_whole(grad_out_theirs)
    gate_halves[0] = cross_planes(gate_halves[0])
    gate_halves[1] = swap(gate_halves[1], "dp", 1 << top)

    inputs = tokens[0].astype(f32)
    mixed_out, _, (gate_halves, down_halves, grad_out_far), _ = scatter_rows(
        mixed_low, out_proj, plainly(dot), (gate_halves, down_halves, grad_out_far)
    )
    middle = inputs + mixed_out
    inv_two = rms_scale(middle)
    normed_two = middle * inv_two
    hidden_two_own = (normed_two * gain_two).astype(bf16)
    gate_halves[1] = cross_planes(gate_halves[1])
    down_halves[0] = cross_planes(down_halves[0])
    hidden_two_near, hidden_two_theirs, gate_halves, down_halves = lax.optimization_barrier(
        (
            gather_whole(hidden_two_own),
            swap(hidden_two_own, "dp", 1 << top),
            gate_halves,
            down_halves,
        ),
    )
    down_halves[1] = cross_planes(down_halves[1])
    gate_mine = join_planes(gate_mine)
    gate_theirs = jnp.concatenate([join_planes(pair) for pair in gate_halves], axis=1)
    down = jnp.concatenate([join_planes(pair) for pair in down_halves], axis=1)
    down = down.reshape(hidden, width)
    hidden_two_far = gather_whole(hidden_two_theirs)
    grad_outs = [grad_out_near, grad_out_far]
    gate = jnp.concatenate(
        [
            jnp.where(side == 0, gate_mine, gate_theirs),
            jnp.where(side == 0, gate_theirs, gate_mine),
        ]
    ).reshape(width, 2 * hidden)

    activation_near, grad_both_near = swiglu(
        dot(hidden_two_near, gate), contract_last(grad_outs[0], down)
    )
    grad_two, _, _, far_inputs = scatter_rows(
        grad_both_near, gate, plainly(contract_last), ahead=(hidden_two_far, grad_outs[1])
    )
    hidden_two_far, grad_outs[1] = far_inputs
    gate_both, grad_two = lax.optimization_barrier((dot(hidden_two_far, gate), grad_two))
    activation_far, grad_both_far = swiglu(gate_both, contract_last(grad_outs[1], down))
    activations = [activation_near, activation_far]
    hidden_twos = [hidden_two_near, hidden_two_far]
    grad_boths = [grad_both_near, grad_both_far]

    def gate_terms(group):
        rows_in_group = width // 2
        terms = sum(
            contract_first(
                lax.dynamic_slice_in_dim(hidden_two, group * rows_in_group, rows_in_group, 1),
                grad_both,
            )
            for hidden_two, grad_both in zip(hidden_twos, grad_boths)
        )
        return terms.astype(bf16).reshape(sharers, ranks * own_rows, 2 * hidden)

    def sum_planes(values):
        for bit in range(top)[::-1]:
            values = halved(values.astype(bf16), "dp", bit)
        return values[0]

    grad_two_far, started, _, _ = scatter_rows(grad_both_far, gate, plainly(contract_last))
    hidden_twos, grad_boths, activations, started = lax.optimization_barrier(
        (hidden_twos, grad_boths, activations, started)
    )
    down_term = sum(contract_first(a, g) for a, g in zip(activations, grad_outs)).astype(bf16)
    term_theirs = sum_planes(gate_terms(1 - side)).astype(bf16)
    grad_two += swap(grad_two_far.astype(bf16), "dp", 1 << top).astype(f32)
    term_mine = gate_terms(side)
    grad_two, term_mine, term_theirs, down_term, activations = lax.optimization_barrier(
        (grad_two, term_mine, term_theirs, down_term, activations)
    )
    theirs_parts = thirds(term_theirs, 0)
    down_parts = thirds(down_term.reshape(sharers, units, width), 1)
    def cross(parts, at):
        theirs, downs = list(parts[0]), list(parts[1])
        theirs[at] = swap(theirs[at], "dp", 1 << top)
        downs[at] = sum_planes(downs[at])
        return theirs, downs

    reduced_two = grad_two * gain_two
    grad_gain_two = jnp.sum(grad_two * normed_two, axis=0)
    grad_after = cotangent[0].astype(f32) + inv_two * (
        reduced_two - normed_two * jnp.mean(reduced_two * normed_two, axis=-1, keepdims=True)
    )
    after_low = gather_whole(grad_after.astype(bf16))
    output_far, _, parts, _ = scatter_rows(
        activations[1],
        down,
        plainly(dot),
        ahead=cross((theirs_parts, down_parts), 0),
        then=lambda parts: cross(parts, 1),
    )
    grad_mixed = contract_last(after_low, out_proj).astype(bf16)
    grad_mixed, mixed_low, after_low, term_mine, parts, output_far = lax.optimization_barrier(
        (grad_mixed, mixed_low, after_low, term_mine, parts, output_far)
    )
    parts = cross(parts, 2)
    term_mine = sum_planes(term_mine).astype(bf16)
    grad_parts = attention_backward(queries, keys, values, grad_mixed, totals, tables)
    grad_parts, term_mine, parts = lax.optimization_barrier((grad_parts, term_mine, parts))
    term_theirs = jnp.concatenate(parts[0])
    down_grad = jnp.concatenate(parts[1])
    grad_proj = jnp.concatenate(grad_parts, axis=1)
    qkv_term = contract_first(hidden_one, grad_proj).astype(bf16)
    out_term = contract_first(mixed_low, after_low).astype(bf16)
    if aligned:
        out_term = out_term.reshape(width, local_width)
        qkv_term = jnp.concatenate([qkv_term, out_term], axis=1)
    else:
        spread = jnp.zeros((local_heads, ranks, HEAD, width), bf16)
        spread = lax.dynamic_update_index_in_dim(
            spread, out_term.reshape(local_heads, 1, HEAD, width), rank, 1
        )
        out_grad = lax.psum_scatter(
            spread.reshape(HEADS * HEAD, width), every, scatter_dimension=0, tiled=True
        )
    grad_proj, qkv_term, inputs_low, activation_near = lax.optimization_barrier(
        (grad_proj, qkv_term, inputs_low, activations[0])
    )
    qkv_term = jnp.concatenate(
        [
            lax.psum_scatter(part, "dp", scatter_dimension=0, tiled=True)
            for part in jnp.split(qkv_term, 2, axis=1)
        ],
        axis=1,
    )
    if aligned:
        out_grad = qkv_term[:, 3 * local_width :].reshape(own_rows, width)
        qkv_term = qkv_term[:, : 3 * local_width]
    out_grad = out_grad.astype(f32)
    gain_one_parts = []

    def gained(*operands):
        product, gain = core_product(*operands, True, (inputs_low, scale_one))
        gain_one_parts.append(gain.reshape(width))
        return product

    grad_one = scatter_rows(grad_proj, qkv, gained)[0]
    grad_gain_one = sum(gain_one_parts)
    inv_one = rms_scale(inputs)
    normed_one = inputs * inv_one
    reduced_one = grad_one * gain_one
    grad_input = grad_after + inv_one * (
        reduced_one - normed_one * jnp.mean(reduced_one * normed_one, axis=-1, keepdims=True)
    )

    output_near = scatter_rows(
        activation_near, down, lambda *operands: core_product(*operands, False)[0]
    )[0]
    term_cols = jnp.stack(
        [
            jnp.where(side == 0, term_mine, term_theirs),
            jnp.where(side == 0, term_theirs, term_mine),
        ]
    )
    term_cols = term_cols.reshape(2, ranks, own_rows, 2 * hidden).transpose(1, 0, 2, 3)
    gate_pieces = exchange(term_cols)
    gain_grad = jnp.stack([grad_gain_one, grad_gain_two]).reshape(2, planes, ranks, -1)
    gain_grad = gain_grad.transpose(2, 1, 0, 3)
    for bit in range(bit_count("ctx"))[::-1]:
        gain_grad = halved(gain_grad, "ctx", bit)
    gate_stepped = gate_step(
        gate_pieces, gate_up, gate_first, gate_second, 3.0 / math.sqrt(D), sharers, units
    )
    down_stepped = plain_step(
        down_grad, down_weight, down_first, down_second, 3.0 / math.sqrt(FF)
    )
    held_back = (gate_stepped, down_stepped, output_near, output_far, grad_input, gain_grad)
    qkv_term, out_grad, held_back = lax.optimization_barrier((qkv_term, out_grad, held_back))
    gate_stepped, down_stepped, output_near, output_far, grad_input, gain_grad = held_back
    gate_grad, gate_new, gate_moment, gate_square = gate_stepped
    down_grad, down_new, down_moment, down_square = down_stepped
    output_far = output_far.astype(bf16)
    gain_parts = [pick(gain_grad[0], plane ^ offset, 0) for offset in range(planes)]
    qkv_pieces, output_far = exchange(
        qkv_term.reshape(ranks, own_rows, 3 * local_width), swap(output_far, "dp", 1 << top)
    )
    gain_parts, output_far = lax.optimization_barrier((gain_parts, output_far))
    outputs = middle + output_near + output_far.astype(f32)
    gain_grad = sum(
        gain_parts[:1]
        + [swap(part, "dp", offset) for offset, part in enumerate(gain_parts) if offset]
    )
    gain_grad = gain_grad.reshape(2, -1)
    attn_grad, attn_new, attn_moment, attn_square = attn_step(
        qkv_pieces, out_grad, attn_weight, attn_first, attn_second, 3.0 / math.sqrt(D)
    )
    gain_new, gain_moment, gain_square = adam_step(
        norm_gains, gain_grad, gain_first, gain_second, gain_rate, 0.0
    )
    return (
        outputs.astype(bf16)[None],
        grad_input.astype(bf16)[None],
        attn_grad,
        gate_grad,
        down_grad,
        gain_grad,
        attn_new,
        gate_new,
        down_new,
        gain_new,
        attn_moment,
        gate_moment,
        down_moment,
        gain_moment,
        attn_square,
        gate_square,
        down_square,
        gain_square,
    )


def solution(mesh):
    acts = P("dp", "ctx", None)
    weight = P(("dp", "ctx"), None)
    gains = P(None, ("dp", "ctx"))
    four = (weight, weight, weight, gains)
    return jax.shard_map(
        body,
        mesh=mesh,
        in_specs=(acts, acts, P()) + four + (weight,) * 6 + (gains,) * 2,
        out_specs=(acts, acts) + four * 4,
        check_vma=False,
    )
```
